32 devices in a mesh: strip: 8 (over y, x, core), dict: 4 (over z).
Axes of the slice: x: 2, y: 2, z: 4, core: 2. Of those that a mesh axis runs over, the one named last changes fastest.
Arguments:
- patterns: bfloat16 [3600, 64, 512], P(None, 'strip', 'dict'), may hold values from -100 to 160
- scan_mask: int32 [64, 512], P('strip', 'dict'), may hold values 0 or 1
- neighbour_mask: int32 [8, 64, 512], P(None, 'strip', 'dict'), may hold values 0 or 1
- dictionary: bfloat16 [2, 512, 3600], P(None, ('strip', 'dict')), may hold values from -160 to 160
Outputs:
- top_scores: float32 [2, 4, 64, 512], P(None, None, 'strip', 'dict')
The draws below stay inside these ranges and needn't reach their ends.
All inputs are finite; a program needn't handle non-finite values. No bound on the sum of `scan_mask` or of `neighbour_mask` on one device may be relied on, other than what follows from the above.
Results may differ from the reference program's by a relative error of at most 0.00081.
Values may be sent and summed in bfloat16 or wider, within the bound.
No kernel may reach another device: no remote copies, remote signals or barrier semaphores. Data moves between devices by JAX's collectives and lax.ppermute only.
A program may use at most 192 MiB of HBM per device.

```python
import math
import jax
import jax.numpy as jnp
from jax import lax

PH = 60
PANELS = 2
ENTRIES = 512
TOP = 4
ROWS_DEV = 8
ROWS = 64
COLS = 512


def dictionary_core(key):
    k_base, k_entry, k_pixel = jax.random.split(jax.random.fold_in(key, 11), 3)
    base_values = jnp.clip(jax.random.normal(k_base, (PANELS * ENTRIES, PH * PH), jnp.float32), -4.0, 4.0)
    pixel_scale = jnp.exp(jax.random.uniform(k_pixel, (1, PH * PH), jnp.float32, 0.0, math.log(4.0)))
    entry_scale = jnp.exp(jax.random.uniform(k_entry, (PANELS * ENTRIES, 1), jnp.float32, 0.0, math.log(10.0)))
    return (base_values * pixel_scale, entry_scale)


def draw_dictionary(key, part):
    unit_rows, entry_scale = dictionary_core(key)
    return (unit_rows * entry_scale).reshape(PANELS, ENTRIES, PH * PH).astype(jnp.bfloat16)


def draw_patterns(key, part):
    unit_rows, entry_scale = dictionary_core(key)
    k_id, k_noise, k_amp, k_back, k_row, k_col = jax.random.split(jax.random.fold_in(key, 23), 6)
    orient_ids = jax.random.randint(k_id, (ROWS, COLS), 0, PANELS * ENTRIES)
    signal_part = jnp.take(unit_rows.T, orient_ids, axis=1) * 0.5
    noise_part = 0.5 * jnp.clip(jax.random.normal(k_noise, (PH * PH, ROWS, COLS), jnp.float32), -4.0, 4.0)
    back_level = jax.random.uniform(k_back, (ROWS, COLS), jnp.float32, 2.0, 6.0)
    amplitude = jnp.exp(jax.random.uniform(k_amp, (ROWS, COLS), jnp.float32, 0.0, math.log(10.0)))
    centre_row = jax.random.uniform(k_row, (ROWS, COLS), jnp.float32, 0.3 * PH, 0.7 * PH)
    centre_col = jax.random.uniform(k_col, (ROWS, COLS), jnp.float32, 0.3 * PH, 0.7 * PH)
    pixel_ids = jnp.arange(PH * PH, dtype=jnp.int32)
    detector_row = (pixel_ids // PH).astype(jnp.float32)[:, None, None]
    detector_col = (pixel_ids % PH).astype(jnp.float32)[:, None, None]
    bump_width = 0.4 * PH
    bump_shape = jnp.exp(-((detector_row - centre_row) ** 2 + (detector_col - centre_col) ** 2) / (2.0 * bump_width * bump_width))
    return (amplitude * (signal_part + noise_part) + back_level * amplitude * bump_shape).astype(jnp.bfloat16)


def touch_ends(result, own_key, smallest, top_value):
    dims = result.shape
    index_at = [jax.random.randint(jax.random.fold_in(own_key, axis), (), 0, dims[axis]) for axis in range(len(dims))]
    result = result.at[tuple(index_at)].set(smallest)
    longest = dims.index(max(dims))
    index_at[longest] = (index_at[longest] + 1) % dims[longest]
    return result.at[tuple(index_at)].set(top_value)


def setup_inputs(seed: int = 0) -> dict:
    splits = jax.random.split(jax.random.key(seed), 5)
    return {
        "patterns": draw_patterns(jax.random.fold_in(splits[4], 71), 0),
        "scan_mask": touch_ends((jax.random.randint(splits[1], (ROWS, COLS), 0, 8) < 7).astype(jnp.int32), jax.random.fold_in(splits[1], 1), 0, 1),
        "neighbour_mask": touch_ends((jax.random.randint(splits[2], (8, ROWS, COLS), 0, 2) < 1).astype(jnp.int32), jax.random.fold_in(splits[2], 1), 0, 1),
        "dictionary": draw_dictionary(jax.random.fold_in(splits[4], 71), 0),
    }


epsilon = 1e-05
nlpar_scale = 2.0

def blur_matrix():
    positions = jnp.arange(PH, dtype=jnp.int32).astype(jnp.float32)
    spread_px = PH / 8.0
    profile = jnp.exp(-(positions[:, None] - positions[None, :]) ** 2 / (2.0 * spread_px * spread_px))
    return (profile / lax.optimization_barrier(jnp.sum(profile, axis=1, keepdims=True))).astype(jnp.bfloat16)

def standardize(row_block, kernel):
    block_shape = row_block.shape
    detector = row_block.reshape(PH, PH, -1).astype(jnp.float32)
    kernel32 = kernel.astype(jnp.float32)
    half_pass = jnp.einsum('abm,db->adm', detector, kernel32).astype(jnp.bfloat16)
    background = jnp.einsum('abm,ea->ebm', half_pass.astype(jnp.float32), kernel32)
    corrected = detector - background
    centre_mean = lax.optimization_barrier(jnp.mean(corrected, axis=(0, 1), keepdims=True))
    centred = corrected - centre_mean
    variance = lax.optimization_barrier(jnp.mean(centred * centred, axis=(0, 1), keepdims=True))
    return (centred / jnp.sqrt(variance + epsilon)).astype(jnp.bfloat16).reshape(block_shape)

def neighbour_average(padded, mask_rows, first_row, first_col, all_rows, all_cols):
    row_count = padded.shape[1] - 2
    col_count = padded.shape[2] - 2
    centre = padded[:, 1:row_count + 1, 1:col_count + 1].astype(jnp.float32)
    row_at = first_row + jnp.arange(row_count, dtype=jnp.int32)
    col_at = first_col + jnp.arange(col_count, dtype=jnp.int32)
    numerator = centre
    weight_sum = jnp.ones((row_count, col_count), jnp.float32)
    slot_index = 0
    for row_step in (-1, 0, 1):
        for col_step in (-1, 0, 1):
            if row_step == 0 and col_step == 0:
                continue
            beside = padded[:, 1 + row_step:1 + row_step + row_count, 1 + col_step:1 + col_step + col_count].astype(jnp.float32)
            differ = centre - beside
            distance = lax.optimization_barrier(jnp.mean(differ * differ, axis=0))
            row_ok = (row_at + row_step >= 0) & (row_at + row_step < all_rows)
            col_ok = (col_at + col_step >= 0) & (col_at + col_step < all_cols)
            usable = row_ok[:, None] & col_ok[None, :] & (mask_rows[slot_index] == 1)
            weight = jnp.where(usable, jnp.exp(-distance / nlpar_scale), jnp.zeros_like(distance))
            numerator = numerator + weight[None] * beside
            weight_sum = weight_sum + weight
            slot_index += 1
    return (numerator / weight_sum[None]).astype(jnp.bfloat16)

def reference(patterns, scan_mask, neighbour_mask, dictionary):
    kernel = blur_matrix()
    masked = patterns * scan_mask.astype(jnp.bfloat16)[None]
    block_count = ROWS // ROWS_DEV
    pixel_count = PH * PH

    def standard_block(index):
        row_block = lax.dynamic_slice_in_dim(masked, index * ROWS_DEV, ROWS_DEV, axis=1)
        return standardize(row_block, kernel)
    stacked = lax.map(standard_block, jnp.arange(block_count, dtype=jnp.int32))
    standard = jnp.moveaxis(stacked, 0, 1).reshape(pixel_count, ROWS, COLS)
    padded = jnp.pad(standard, ((0, 0), (1, 1), (1, 1)))
    dictionary32 = dictionary.astype(jnp.float32)
    inv_entry = 1.0 / jnp.sqrt(lax.optimization_barrier(jnp.mean(dictionary32 * dictionary32, axis=2)) + epsilon)

    def score_rows(index):
        first_row = index * ROWS_DEV
        window = lax.dynamic_slice_in_dim(padded, first_row, ROWS_DEV + 2, axis=1)
        mask_rows = lax.dynamic_slice_in_dim(neighbour_mask, first_row, ROWS_DEV, axis=1)
        averaged = neighbour_average(window, mask_rows, first_row, 0, ROWS, COLS)
        columns = averaged.reshape(pixel_count, -1).astype(jnp.float32)
        inv_pattern = 1.0 / jnp.sqrt(lax.optimization_barrier(jnp.mean(columns * columns, axis=0)) + epsilon)
        products = jnp.einsum('kep,pm->kem', dictionary32, columns)
        scores = products / pixel_count * inv_entry[:, :, None] * inv_pattern[None, None, :]
        ranked = -jnp.sort(-scores, axis=1)[:, :TOP]
        return ranked.reshape(PANELS, TOP, ROWS_DEV, COLS)
    ranked_all = lax.map(score_rows, jnp.arange(block_count, dtype=jnp.int32))
    return jnp.moveaxis(ranked_all, 0, 2).reshape(PANELS, TOP, ROWS, COLS)
```

```python
import functools

import jax
import jax.numpy as jnp
import ml_dtypes
import numpy as np
from jax import lax
from jax.experimental import pallas as pl
from jax.experimental.pallas import tpu as pltpu
from jax.sharding import PartitionSpec as P

PH = 60
TOP = 4
QUAD = 4
GROUPS = PH // QUAD
TILE = QUAD * QUAD
CHUNK = GROUPS * TILE
DEPTH = 256
LANES = 128
SIDES = 32

epsilon = 1e-05
nlpar_scale = 2.0
MIB = 1 << 20


def blur_matrix():
    at = np.arange(PH, dtype=np.float32)
    spread_px = np.float32(PH / 8.0)
    gap = at[:, None] - at[None, :]
    profile = np.exp(-(gap * gap) / (np.float32(2.0) * spread_px * spread_px))
    profile = profile / profile.sum(axis=1, keepdims=True)
    return profile.astype(ml_dtypes.bfloat16).astype(np.float32)


def pass_matrices():
    kernel = blur_matrix()
    index = np.arange(CHUNK)
    quad, row, col = index // TILE, (index // QUAD) % QUAD, index % QUAD
    along = quad * QUAD + col
    columns = kernel[along[:, None], along[None, :]] * (row[:, None] == row[None, :])
    down = quad * QUAD + row
    rows = kernel[down[:, None], down[None, :]] * (col[:, None] == col[None, :])
    natural = row * PH + along
    order = (index[:, None] == natural[None, :]).astype(np.float32)
    out = np.zeros((3, CHUNK, DEPTH), np.float32)
    out[0, :, :CHUNK], out[1, :, :CHUNK], out[2, :, :CHUNK] = columns, rows, order
    return out.astype(ml_dtypes.bfloat16)


def tiles_of(pieces):
    return jnp.concatenate(pieces + [pieces[-1]], axis=0)


def standardize_kernel(x_hbm, mask_ref, mat_ref, s_ref, raw, xq, half, corr, sq, sems):
    pair = pl.program_id(0)

    @pl.when(pair == 0)
    def _():
        def fetch(g):
            return pltpu.make_async_copy(x_hbm.at[pl.ds(g * CHUNK, CHUNK)], raw.at[g], sems.at[g])

        for g in range(GROUPS):
            fetch(g).start()
        mask = mask_ref[...].astype(jnp.bfloat16)[None]

        for g in range(GROUPS):
            fetch(g).wait()
            for quad in range(GROUPS):
                piece = jnp.concatenate(
                    [raw[g, pl.ds(row * PH + quad * QUAD, QUAD)] for row in range(QUAD)], axis=0
                )
                xq[:, quad, pl.ds(g * TILE, TILE), :] = jnp.swapaxes(piece * mask, 0, 1)

    r0 = pair * 2

    def both(quad, rows):
        return jnp.concatenate([xq[r0, quad, rows, :], xq[r0 + 1, quad, rows, :]], axis=1)

    for g in range(GROUPS):
        rhs = tiles_of([both(quad, pl.ds(g * TILE, TILE)) for quad in range(GROUPS)])
        out = jnp.dot(mat_ref[0], rhs, preferred_element_type=jnp.float32)
        half[g] = out.astype(jnp.bfloat16)

    total = jnp.zeros((8, 2 * LANES), jnp.float32)
    squares = jnp.zeros((8, 2 * LANES), jnp.float32)
    for quad in range(GROUPS):
        rhs = tiles_of([half[g, pl.ds(quad * TILE, TILE), :] for g in range(GROUPS)])
        background = jnp.dot(mat_ref[1], rhs, preferred_element_type=jnp.float32)
        corrected = both(quad, slice(None)).astype(jnp.float32) - background
        corr[quad] = corrected
        folded = corrected.reshape(CHUNK // 8, 8, 2 * LANES)
        total = total + jnp.sum(folded, axis=0)
        squares = squares + jnp.sum(folded * folded, axis=0)
    pixels = GROUPS * CHUNK
    mean = jnp.sum(total, axis=0, keepdims=True) / pixels
    variance = jnp.sum(squares, axis=0, keepdims=True) / pixels - mean * mean
    scale = 1.0 / jnp.sqrt(jnp.maximum(variance, 0.0) + epsilon)
    for quad in range(GROUPS):
        sq[quad] = ((corr[quad] - mean) * scale).astype(jnp.bfloat16)
    for g in range(GROUPS):
        rhs = tiles_of([sq[quad, pl.ds(g * TILE, TILE), :] for quad in range(GROUPS)])
        out = jnp.dot(mat_ref[2], rhs, preferred_element_type=jnp.float32).astype(jnp.bfloat16)
        s_ref[0, pl.ds(g * CHUNK, CHUNK), :] = out[:, :LANES]
        s_ref[1, pl.ds(g * CHUNK, CHUNK), :] = out[:, LANES:]


def standardize(patterns, scan_mask):
    pixels, rows, cols = patterns.shape
    return pl.pallas_call(
        standardize_kernel,
        grid=(rows // 2,),
        in_specs=[
            pl.BlockSpec(memory_space=pl.ANY),
            pl.BlockSpec((rows, cols), lambda i: (0, 0)),
            pl.BlockSpec((3, CHUNK, DEPTH), lambda i: (0, 0, 0)),
        ],
        out_specs=pl.BlockSpec((2, pixels, cols), lambda i: (i, 0, 0)),
        out_shape=jax.ShapeDtypeStruct((rows, pixels, cols), jnp.bfloat16),
        scratch_shapes=[
            pltpu.VMEM((GROUPS, CHUNK, rows, cols), jnp.bfloat16),
            pltpu.VMEM((rows, GROUPS, CHUNK, cols), jnp.bfloat16),
            pltpu.VMEM((GROUPS, CHUNK, 2 * cols), jnp.bfloat16),
            pltpu.VMEM((GROUPS, CHUNK, 2 * cols), jnp.float32),
            pltpu.VMEM((GROUPS, CHUNK, 2 * cols), jnp.bfloat16),
            pltpu.SemaphoreType.DMA((GROUPS,)),
        ],
        compiler_params=pltpu.CompilerParams(vmem_limit_bytes=48 * MIB),
        cost_estimate=pl.CostEstimate(
            flops=6_000_000_000, bytes_accessed=15_000_000, transcendentals=0
        ),
        name="standardize",
    )(patterns, scan_mask, jnp.asarray(pass_matrices()))


def edges_kernel(s_ref, o_ref):
    rows = s_ref.shape[0]
    at_row = lax.broadcasted_iota(jnp.int32, (2 * rows, 2 * LANES), 0)
    at_lane = lax.broadcasted_iota(jnp.int32, (2 * rows, 2 * LANES), 1)
    for g in range(GROUPS):
        span = pl.ds(g * CHUNK, CHUNK)
        out = jnp.zeros((2 * rows, CHUNK), jnp.float32)
        for r in range(0, rows, 2):
            wanted = jnp.where(at_row < rows, 0, LANES - 1)
            row = jnp.where(at_row < rows, at_row, at_row - rows)
            pick = (at_lane == wanted + (row - r) * LANES).astype(jnp.bfloat16)
            block = jnp.concatenate([s_ref[r, span, :], s_ref[r + 1, span, :]], axis=1)
            out = out + lax.dot_general(
                pick, block, (((1,), (1,)), ((), ())), preferred_element_type=jnp.float32
            )
        o_ref[:, g * CHUNK : (g + 1) * CHUNK] = out.astype(jnp.bfloat16)


def edges(standard):
    rows, pixels, _ = standard.shape
    return pl.pallas_call(
        edges_kernel,
        out_shape=jax.ShapeDtypeStruct((2 * rows, pixels), jnp.bfloat16),
        compiler_params=pltpu.CompilerParams(vmem_limit_bytes=48 * MIB),
        name="edges",
    )(standard)


def diagonals(product, at_sub, at_lane):
    return [
        jnp.sum(jnp.where(at_sub == at_lane + d, product, 0.0), axis=0, keepdims=True)
        for d in (-1, 0, 1)
    ]


def average_kernel(s_ref, top_ref, bottom_ref, side_ref, usable_ref, a_ref, inv_ref, sides, weights):
    rows, pixels, cols = s_ref.shape
    f32 = jnp.float32
    at_sub = lax.broadcasted_iota(jnp.int32, (cols, cols), 0)
    at_lane = lax.broadcasted_iota(jnp.int32, (cols, cols), 1)
    lane = lax.broadcasted_iota(jnp.int32, (1, cols), 1)

    def row_ref(r):
        return top_ref if r < 0 else bottom_ref if r >= rows else s_ref.at[r]

    side32 = side_ref[...].astype(f32)
    side_norm = jnp.sum(side32 * side32, axis=1, keepdims=True)
    pad = jnp.concatenate([side32, jnp.zeros((cols - SIDES, pixels), f32)], axis=0)
    for start in range(0, pixels, LANES):
        width = min(LANES, pixels - start)
        sides[pl.ds(start, width), :] = pad[:, start : start + width].T.astype(jnp.bfloat16)

    norm, to_next, to_self, to_side = {}, {}, {}, {}
    for r in range(-1, rows + 1):
        here = row_ref(r)[...]
        here32 = here.astype(f32)
        norm[r] = jnp.sum(here32 * here32, axis=0, keepdims=True)
        if r < rows:
            nxt = row_ref(r + 1)[...]
            both = jnp.concatenate([here, nxt], axis=1)
            product = lax.dot_general(here, both, (((0,), (0,)), ((), ())), preferred_element_type=f32)
            to_next[r] = diagonals(product[:, cols:], at_sub, at_lane)
            to_self[r] = diagonals(product[:, :cols], at_sub, at_lane)
        if 0 <= r < rows:
            to_side[r] = jnp.dot(side_ref[...], here, preferred_element_type=f32)

    def shifted(vector, dc):
        if dc == 0:
            return vector
        return pltpu.roll(vector, (-dc) % cols, 1)

    for r in range(rows):
        weight = {}
        slot = 0
        total = jnp.ones((1, cols), f32)
        for dr in (-1, 0, 1):
            for dc in (-1, 0, 1):
                if dr == 0 and dc == 0:
                    continue
                if dr == -1:
                    dot = to_next[r - 1][dc + 1]
                elif dr == 1:
                    dot = shifted(to_next[r][-dc + 1], dc)
                else:
                    dot = to_self[r][0] if dc == -1 else shifted(to_self[r][0], 1)
                other = shifted(norm[r + dr], dc)
                if dc != 0:
                    k = r + dr + 1 + (0 if dc < 0 else 16)
                    end = 0 if dc < 0 else cols - 1
                    dot = jnp.where(lane == end, to_side[r][k : k + 1, :], dot)
                    other = jnp.where(lane == end, side_norm[k : k + 1, :], other)
                distance = jnp.maximum(norm[r] + other - 2.0 * dot, 0.0) / pixels
                weight[dr, dc] = usable_ref[slot, pl.ds(r, 1), :] * jnp.exp(-distance / nlpar_scale)
                total = total + weight[dr, dc]
                slot += 1
        for dr in (-1, 0, 1):
            block = jnp.zeros((cols, cols), f32)
            for dc in (-1, 0, 1):
                w = jnp.ones((1, cols), f32) if dr == 0 and dc == 0 else weight[dr, dc]
                block = jnp.where(at_sub == at_lane + dc, w, block)
            weights[r, dr + 1] = block
        block = jnp.zeros((cols, cols), f32)
        for dr in (-1, 0, 1):
            for dc in (-1, 1):
                k = r + dr + 1 + (0 if dc < 0 else 16)
                end = 0 if dc < 0 else cols - 1
                block = jnp.where((at_sub == k) & (at_lane == end), weight[dr, dc], block)
        weights[r, 3] = block

        full = weights[r].reshape(4 * cols, cols)
        high = full.astype(jnp.bfloat16)
        low = (full - high.astype(f32)).astype(jnp.bfloat16)
        split = jnp.concatenate([high, low], axis=1)
        inverse = 1.0 / total
        squares = jnp.zeros((8, cols), f32)
        for g in range(GROUPS):
            span = pl.ds(g * CHUNK, CHUNK)
            lhs = jnp.concatenate(
                [row_ref(r - 1)[span, :], row_ref(r)[span, :], row_ref(r + 1)[span, :], sides[span, :]],
                axis=1,
            )
            out = jnp.dot(lhs, split, preferred_element_type=f32)
            mean = ((out[:, :cols] + out[:, cols:]) * inverse).astype(jnp.bfloat16)
            a_ref[r, span, :] = mean
            mean32 = mean.astype(f32).reshape(CHUNK // 8, 8, cols)
            squares = squares + jnp.sum(mean32 * mean32, axis=0)
        energy = jnp.sum(squares, axis=0, keepdims=True) / pixels
        inv_ref[pl.ds(r, 1), :] = 1.0 / jnp.sqrt(energy + epsilon)


def average(standard, top, bottom, side, usable):
    rows, pixels, cols = standard.shape
    return pl.pallas_call(
        average_kernel,
        out_shape=(
            jax.ShapeDtypeStruct((rows, pixels, cols), jnp.bfloat16),
            jax.ShapeDtypeStruct((rows, cols), jnp.float32),
        ),
        scratch_shapes=[
            pltpu.VMEM((pixels, cols), jnp.bfloat16),
            pltpu.VMEM((rows, 4, cols, cols), jnp.float32),
        ],
        compiler_params=pltpu.CompilerParams(vmem_limit_bytes=48 * MIB),
        cost_estimate=pl.CostEstimate(
            flops=12_000_000_000, bytes_accessed=17_000_000, transcendentals=0
        ),
        name="average",
    )(standard, top, bottom, side, usable)


def insert(best, new):
    kept = []
    for slot, held in enumerate(best):
        kept.append(jnp.maximum(held, new))
        if slot < len(best) - 1:
            new = jnp.minimum(held, new)
    return kept


def merge_sublanes(best):
    for shift in (4, 2, 1):
        other = [pltpu.roll(b, shift, 0) for b in best]
        m = [jnp.maximum(best[i], other[3 - i]) for i in range(4)]
        a, c = jnp.maximum(m[0], m[2]), jnp.minimum(m[0], m[2])
        b, d = jnp.maximum(m[1], m[3]), jnp.minimum(m[1], m[3])
        best = [jnp.maximum(a, b), jnp.minimum(a, b), jnp.maximum(c, d), jnp.minimum(c, d)]
    return best


def score_kernel(d_ref, a_ref, inv_ref, o_ref, best):
    chunk, chunks = pl.program_id(1), pl.num_programs(1)
    rows, pixels, cols = a_ref.shape
    f32 = jnp.float32

    @pl.when(chunk == 0)
    def _():
        best[...] = jnp.full(best.shape, -jnp.inf, f32)

    entries = d_ref[0]
    entries32 = entries.astype(f32)
    energy = jnp.sum(entries32 * entries32, axis=1, keepdims=True) / pixels
    inv_entry = 1.0 / jnp.sqrt(energy + epsilon)
    for r in range(0, rows, 2):
        block = jnp.concatenate([a_ref[r], a_ref[r + 1]], axis=1)
        products = jnp.dot(entries, block, preferred_element_type=f32)
        scores = products / pixels * inv_entry
        for half in range(2):
            held = [best[j, r + half] for j in range(TOP)]
            for e in range(0, entries.shape[0], 8):
                held = insert(held, scores[e : e + 8, half * cols : (half + 1) * cols])
            for j in range(TOP):
                best[j, r + half] = held[j]

    @pl.when(chunk == chunks - 1)
    def _():
        for r in range(rows):
            held = merge_sublanes([best[j, r] for j in range(TOP)])
            for j in range(TOP):
                o_ref[0, j, pl.ds(r, 1), :] = held[j][:1] * inv_ref[pl.ds(r, 1), :]


def score(dictionary, averaged, inv_pattern, size=128):
    panels, entries, pixels = dictionary.shape
    rows, _, cols = averaged.shape
    return pl.pallas_call(
        score_kernel,
        grid=(panels, entries // size),
        in_specs=[
            pl.BlockSpec((1, size, pixels), lambda k, i: (k, i, 0)),
            pl.BlockSpec((rows, pixels, cols), lambda k, i: (0, 0, 0), pipeline_mode=pl.Buffered(1)),
            pl.BlockSpec((rows, cols), lambda k, i: (0, 0)),
        ],
        out_specs=pl.BlockSpec((1, TOP, rows, cols), lambda k, i: (k, 0, 0, 0)),
        out_shape=jax.ShapeDtypeStruct((panels, TOP, rows, cols), jnp.float32),
        scratch_shapes=[pltpu.VMEM((TOP, rows, 8, cols), jnp.float32)],
        compiler_params=pltpu.CompilerParams(vmem_limit_bytes=48 * MIB),
        cost_estimate=pl.CostEstimate(
            flops=7_500_000_000, bytes_accessed=15_000_000, transcendentals=0
        ),
        name="score",
    )(dictionary, averaged, inv_pattern)


def from_low(x, axis):
    count = lax.axis_size(axis)
    return lax.ppermute(x, axis, [(i, i + 1) for i in range(count - 1)])


def from_high(x, axis):
    count = lax.axis_size(axis)
    return lax.ppermute(x, axis, [(i + 1, i) for i in range(count - 1)])


def usable_neighbours(neighbour_mask):
    _, rows, cols = neighbour_mask.shape
    row_at = lax.axis_index("strip") * rows + jnp.arange(rows, dtype=jnp.int32)
    col_at = lax.axis_index("dict") * cols + jnp.arange(cols, dtype=jnp.int32)
    all_rows = rows * lax.axis_size("strip")
    all_cols = cols * lax.axis_size("dict")
    inside = []
    for dr in (-1, 0, 1):
        for dc in (-1, 0, 1):
            if dr == 0 and dc == 0:
                continue
            row_ok = (row_at + dr >= 0) & (row_at + dr < all_rows)
            col_ok = (col_at + dc >= 0) & (col_at + dc < all_cols)
            inside.append(row_ok[:, None] & col_ok[None, :])
    return (jnp.stack(inside) & (neighbour_mask == 1)).astype(jnp.float32)


def on_device(patterns, scan_mask, neighbour_mask, dictionary):
    rows = patterns.shape[1]
    portion = lax.all_gather(dictionary, ("strip", "dict"), axis=1, tiled=True)
    usable = usable_neighbours(neighbour_mask)
    standard = standardize(patterns, scan_mask)
    top = from_low(standard[rows - 1], "strip")
    bottom = from_high(standard[0], "strip")
    own = edges(standard)
    left = from_low(own, "dict")[rows:]
    right = from_high(own, "dict")[:rows]
    ends = jnp.concatenate([left, right], axis=0)
    above = from_low(ends, "strip")
    below = from_high(ends, "strip")
    blank = jnp.zeros((16 - rows - 2, own.shape[1]), own.dtype)
    side = jnp.concatenate(
        [
            above[rows - 1 : rows], left, below[:1], blank,
            above[2 * rows - 1 :], right, below[rows : rows + 1], blank,
        ],
        axis=0,
    )
    averaged, inv_pattern = average(standard, top, bottom, side, usable)
    return score(portion, averaged, inv_pattern)


def solution(mesh):
    in_specs = (
        P(None, "strip", "dict"),
        P("strip", "dict"),
        P(None, "strip", "dict"),
        P(None, ("strip", "dict"), None),
    )
    out_specs = P(None, None, "strip", "dict")
    return jax.shard_map(
        on_device, mesh=mesh, in_specs=in_specs, out_specs=out_specs, check_vma=False
    )
```

```python
import functools

import jax
import jax.numpy as jnp
import ml_dtypes
import numpy as np
from jax import lax
from jax.experimental import pallas as pl
from jax.experimental.pallas import tpu as pltpu
from jax.sharding import PartitionSpec as P

PH = 60
TOP = 4
QUAD = 4
GROUPS = PH // QUAD
TILE = QUAD * QUAD
CHUNK = GROUPS * TILE
DEPTH = 256
LANES = 128
SIDES = 32

epsilon = 1e-05
nlpar_scale = 2.0
MIB = 1 << 20


def blur_matrix():
    at = np.arange(PH, dtype=np.float32)
    spread_px = np.float32(PH / 8.0)
    gap = at[:, None] - at[None, :]
    profile = np.exp(-(gap * gap) / (np.float32(2.0) * spread_px * spread_px))
    profile = profile / profile.sum(axis=1, keepdims=True)
    return profile.astype(ml_dtypes.bfloat16).astype(np.float32)


def pass_matrices():
    kernel = blur_matrix()
    index = np.arange(CHUNK)
    quad, row, col = index // TILE, (index // QUAD) % QUAD, index % QUAD
    along = quad * QUAD + col
    columns = kernel[along[:, None], along[None, :]] * (row[:, None] == row[None, :])
    down = quad * QUAD + row
    rows = kernel[down[:, None], down[None, :]] * (col[:, None] == col[None, :])
    natural = row * PH + along
    order = (index[:, None] == natural[None, :]).astype(np.float32)
    out = np.zeros((3, CHUNK, DEPTH), np.float32)
    out[0, :, :CHUNK], out[1, :, :CHUNK], out[2, :, :CHUNK] = columns, rows, order
    return out.astype(ml_dtypes.bfloat16)


def tiles_of(pieces):
    return jnp.concatenate(pieces + [pieces[-1]], axis=0)


def on_chip(x):
    return pltpu.with_memory_space_constraint(x, pltpu.VMEM)


def in_hbm(x):
    return pltpu.with_memory_space_constraint(x, pltpu.HBM)


WHOLE = pl.BlockSpec(memory_space=pltpu.VMEM)
APART = pl.BlockSpec(memory_space=pl.ANY)
SHORT = pl.CostEstimate(flops=1000, bytes_accessed=1000, transcendentals=0)
TOKEN = jax.ShapeDtypeStruct((8, LANES), jnp.float32)


def mark(ref):
    ref[...] = jnp.zeros(ref.shape, ref.dtype)


def standard_rows(both, mat_ref, half, corr, sq, stores):
    for g in range(GROUPS):
        rhs = tiles_of([both(quad, slice(g * TILE, (g + 1) * TILE)) for quad in range(GROUPS)])
        out = jnp.dot(mat_ref[0], rhs, preferred_element_type=jnp.float32)
        half[g] = out.astype(jnp.bfloat16)

    total = jnp.zeros((8, 2 * LANES), jnp.float32)
    squares = jnp.zeros((8, 2 * LANES), jnp.float32)
    for quad in range(GROUPS):
        rhs = tiles_of([half[g, pl.ds(quad * TILE, TILE), :] for g in range(GROUPS)])
        background = jnp.dot(mat_ref[1], rhs, preferred_element_type=jnp.float32)
        corrected = both(quad, slice(None)).astype(jnp.float32) - background
        corr[quad] = corrected
        folded = corrected.reshape(CHUNK // 8, 8, 2 * LANES)
        total = total + jnp.sum(folded, axis=0)
        squares = squares + jnp.sum(folded * folded, axis=0)
    pixels = GROUPS * CHUNK
    mean = jnp.sum(total, axis=0, keepdims=True) / pixels
    variance = jnp.sum(squares, axis=0, keepdims=True) / pixels - mean * mean
    scale = 1.0 / jnp.sqrt(jnp.maximum(variance, 0.0) + epsilon)
    for quad in range(GROUPS):
        sq[quad] = ((corr[quad] - mean) * scale).astype(jnp.bfloat16)
    for g in range(GROUPS):
        rhs = tiles_of([sq[quad, pl.ds(g * TILE, TILE), :] for quad in range(GROUPS)])
        out = jnp.dot(mat_ref[2], rhs, preferred_element_type=jnp.float32).astype(jnp.bfloat16)
        for side, store in enumerate(stores):
            store(slice(g * CHUNK, (g + 1) * CHUNK), out[:, side * LANES : (side + 1) * LANES])


def border_kernel(x_hbm, mask_hbm, mat_hbm, xq_hbm, first, last, token, mask_ref, mat_ref, xq, ends, raw, half, corr, sq, sems):
    rows = raw.shape[2]
    mark(token)

    def fetch(g):
        return pltpu.make_async_copy(x_hbm.at[pl.ds(g * CHUNK, CHUNK)], raw.at[g], sems.at[g])

    mask_copy = pltpu.make_async_copy(mask_hbm, mask_ref, sems.at[GROUPS])
    matrices = pltpu.make_async_copy(mat_hbm, mat_ref, sems.at[GROUPS + 1])
    keep = pltpu.make_async_copy(xq, xq_hbm, sems.at[GROUPS + 2])
    mask_copy.start()
    for g in range(GROUPS):
        fetch(g).start()
    matrices.start()
    mask_copy.wait()
    mask = mask_ref[...].astype(jnp.bfloat16)[None]
    for g in range(GROUPS):
        fetch(g).wait()
        for quad in range(GROUPS):
            piece = jnp.concatenate(
                [raw[g, pl.ds(row * PH + quad * QUAD, QUAD)] for row in range(QUAD)], axis=0
            )
            tile = jnp.swapaxes(piece * mask, 0, 1)
            span = slice(g * TILE, (g + 1) * TILE)
            xq[:, quad, span, :] = tile[1 : rows - 1]
            ends[0, quad, span, :] = tile[0]
            ends[1, quad, span, :] = tile[rows - 1]
    keep.start()
    matrices.wait()

    def both(quad, span):
        return jnp.concatenate([ends[0, quad, span, :], ends[1, quad, span, :]], axis=1)

    def store(ref):
        def put(span, value):
            ref[span, :] = value

        return put

    standard_rows(both, mat_ref, half, corr, sq, [store(first), store(last)])
    keep.wait()


def row_scratch(cols):
    return [
        pltpu.VMEM((GROUPS, CHUNK, 2 * cols), jnp.bfloat16),
        pltpu.VMEM((GROUPS, CHUNK, 2 * cols), jnp.float32),
        pltpu.VMEM((GROUPS, CHUNK, 2 * cols), jnp.bfloat16),
    ]


def border(patterns, scan_mask, matrices):
    pixels, rows, cols = patterns.shape
    bf16 = jnp.bfloat16
    return pl.pallas_call(
        border_kernel,
        in_specs=[APART] * 3,
        out_specs=(APART, WHOLE, WHOLE, WHOLE),
        out_shape=(
            pltpu.HBM((rows - 2, GROUPS, CHUNK, cols), bf16),
            pltpu.VMEM((pixels, cols), bf16),
            pltpu.VMEM((pixels, cols), bf16),
            TOKEN,
        ),
        scratch_shapes=[
            pltpu.VMEM((rows, cols), scan_mask.dtype),
            pltpu.VMEM(matrices.shape, bf16),
            pltpu.VMEM((rows - 2, GROUPS, CHUNK, cols), bf16),
            pltpu.VMEM((2, GROUPS, CHUNK, cols), bf16),
            pltpu.VMEM((GROUPS, CHUNK, rows, cols), bf16),
        ]
        + row_scratch(cols)
        + [pltpu.SemaphoreType.DMA((GROUPS + 3,))],
        compiler_params=pltpu.CompilerParams(vmem_limit_bytes=26 * MIB),
        cost_estimate=SHORT,
        name="border",
    )(in_hbm(patterns), in_hbm(scan_mask), in_hbm(matrices))


def interior_kernel(xq_hbm, mat_hbm, _, s_ref, token, mat_ref, xq, half, corr, sq, sems):
    mark(token)
    pairs = s_ref.shape[0] // 2
    matrices = pltpu.make_async_copy(mat_hbm, mat_ref, sems.at[2])

    def fetch(i, slot):
        return pltpu.make_async_copy(xq_hbm.at[pl.ds(2 * i, 2)], xq.at[slot], sems.at[slot])

    fetch(0, 0).start()
    matrices.start()
    matrices.wait()

    def pair(i, carry):
        slot = lax.rem(i, 2)
        fetch(i, slot).wait()

        @pl.when(i + 1 < pairs)
        def _():
            fetch(i + 1, 1 - slot).start()

        def both(quad, span):
            return jnp.concatenate([xq[slot, 0, quad, span, :], xq[slot, 1, quad, span, :]], axis=1)

        def store(side):
            def put(span, value):
                s_ref[2 * i + side, span, :] = value

            return put

        standard_rows(both, mat_ref, half, corr, sq, [store(0), store(1)])
        return carry

    lax.fori_loop(0, pairs, pair, 0)


def interior(xq, matrices, earlier):
    rows, _, _, cols = xq.shape
    pixels = GROUPS * CHUNK
    return pl.pallas_call(
        interior_kernel,
        in_specs=[APART, APART, WHOLE],
        out_specs=(WHOLE, WHOLE),
        out_shape=(pltpu.VMEM((rows, pixels, cols), jnp.bfloat16), TOKEN),
        scratch_shapes=[
            pltpu.VMEM(matrices.shape, jnp.bfloat16),
            pltpu.VMEM((2, 2, GROUPS, CHUNK, cols), jnp.bfloat16),
        ]
        + row_scratch(cols)
        + [pltpu.SemaphoreType.DMA((3,))],
        compiler_params=pltpu.CompilerParams(vmem_limit_bytes=16 * MIB),
        cost_estimate=SHORT,
        name="interior",
    )(in_hbm(xq), in_hbm(matrices), earlier)


def row_of(refs, rows):
    above, first, middle, last, below = refs

    def row(r):
        if 1 <= r < rows - 1:
            return middle.at[r - 1]
        return {-1: above, 0: first, rows - 1: last, rows: below}[r]

    return row


def diagonals(product, at_sub, at_lane):
    return [
        jnp.sum(jnp.where(at_sub == at_lane + d, product, 0.0), axis=0, keepdims=True)
        for d in (-1, 0, 1)
    ]


PER_ROW = 8


def products_kernel(*refs):
    left, right, out = refs[-3:]
    rows = refs[2].shape[0] + 2
    row = row_of(refs[:5], rows)
    cols = refs[0].shape[1]
    f32 = jnp.float32
    at_sub = lax.broadcasted_iota(jnp.int32, (cols, cols), 0)
    at_lane = lax.broadcasted_iota(jnp.int32, (cols, cols), 1)
    firsts, lasts = [], []
    for r in range(-1, rows + 1):
        here = row(r)[...]
        across = here.T
        firsts.append(across[:1])
        lasts.append(across[cols - 1 :])
        pieces = [here]
        if r < rows:
            pieces.append(row(r + 1)[...])
        product = jnp.dot(across, jnp.concatenate(pieces, axis=1), preferred_element_type=f32)
        own = diagonals(product[:, :cols], at_sub, at_lane)
        vectors = [own[1], own[0]]
        if r < rows:
            vectors += diagonals(product[:, cols:], at_sub, at_lane)
        vectors += [jnp.zeros((1, cols), f32)] * (PER_ROW - len(vectors))
        out[r + 1] = jnp.concatenate(vectors, axis=0)
    blank = [jnp.zeros((SIDES // 2 - len(firsts), here.shape[0]), firsts[0].dtype)]
    left[...] = jnp.concatenate(firsts + blank, axis=0)
    right[...] = jnp.concatenate(lasts + blank, axis=0)


def products(block, *earlier):
    rows = block[2].shape[0] + 2
    pixels, cols = block[0].shape
    one = jax.ShapeDtypeStruct((SIDES // 2, pixels), jnp.bfloat16)
    return pl.pallas_call(
        products_kernel,
        in_specs=[WHOLE] * (5 + len(earlier)),
        out_specs=(WHOLE,) * 3,
        out_shape=(one, one, jax.ShapeDtypeStruct((rows + 2, PER_ROW, cols), jnp.float32)),
        compiler_params=pltpu.CompilerParams(vmem_limit_bytes=12 * MIB),
        cost_estimate=SHORT,
        name="products",
    )(*map(on_chip, block), *earlier)


def average_kernel(*refs):
    left_ref, right_ref, dot_ref, usable_ref = refs[5:9]
    a_ref, inv_ref, sides, weights = refs[-4:]
    rows, pixels, cols = a_ref.shape
    row = row_of(refs[:5], rows)
    f32 = jnp.float32
    at_sub = lax.broadcasted_iota(jnp.int32, (cols, cols), 0)
    at_lane = lax.broadcasted_iota(jnp.int32, (cols, cols), 1)
    lane = lax.broadcasted_iota(jnp.int32, (1, cols), 1)

    side = jnp.concatenate([left_ref[...], right_ref[...]], axis=0)
    side32 = side.astype(f32)
    side_norm = jnp.sum(side32 * side32, axis=1, keepdims=True)
    pad = jnp.concatenate([side32, jnp.zeros((cols - SIDES, pixels), f32)], axis=0)
    for start in range(0, pixels, LANES):
        width = min(LANES, pixels - start)
        sides[pl.ds(start, width), :] = pad[:, start : start + width].T.astype(jnp.bfloat16)

    def shifted(vector, dc):
        if dc == 0:
            return vector
        return pltpu.roll(vector, (-dc) % cols, 1)

    def kept(r, k):
        return dot_ref[r + 1, pl.ds(k, 1), :]

    for r in range(rows):
        to_side = jnp.dot(side, row(r)[...], preferred_element_type=f32)
        weight = {}
        slot = 0
        total = jnp.ones((1, cols), f32)
        for dr in (-1, 0, 1):
            for dc in (-1, 0, 1):
                if dr == 0 and dc == 0:
                    continue
                if dr == -1:
                    dot = kept(r - 1, 3 + dc)
                elif dr == 1:
                    dot = shifted(kept(r, 3 - dc), dc)
                else:
                    dot = kept(r, 1) if dc == -1 else shifted(kept(r, 1), 1)
                other = shifted(kept(r + dr, 0), dc)
                if dc != 0:
                    k = r + dr + 1 + (0 if dc < 0 else 16)
                    end = 0 if dc < 0 else cols - 1
                    dot = jnp.where(lane == end, to_side[k : k + 1, :], dot)
                    other = jnp.where(lane == end, side_norm[k : k + 1, :], other)
                distance = jnp.maximum(kept(r, 0) + other - 2.0 * dot, 0.0) / pixels
                weight[dr, dc] = usable_ref[slot, pl.ds(r, 1), :] * jnp.exp(-distance / nlpar_scale)
                total = total + weight[dr, dc]
                slot += 1
        for dr in (-1, 0, 1):
            block = jnp.zeros((cols, cols), f32)
            for dc in (-1, 0, 1):
                w = jnp.ones((1, cols), f32) if dr == 0 and dc == 0 else weight[dr, dc]
                block = jnp.where(at_sub == at_lane + dc, w, block)
            weights[dr + 1] = block
        block = jnp.zeros((cols, cols), f32)
        for dr in (-1, 0, 1):
            for dc in (-1, 1):
                k = r + dr + 1 + (0 if dc < 0 else 16)
                end = 0 if dc < 0 else cols - 1
                block = jnp.where((at_sub == k) & (at_lane == end), weight[dr, dc], block)
        weights[3] = block

        full = weights[...].reshape(4 * cols, cols)
        high = full.astype(jnp.bfloat16)
        low = (full - high.astype(f32)).astype(jnp.bfloat16)
        split = jnp.concatenate([high, low], axis=1)
        inverse = 1.0 / total
        squares = jnp.zeros((8, cols), f32)
        for g in range(GROUPS):
            span = slice(g * CHUNK, (g + 1) * CHUNK)
            lhs = jnp.concatenate(
                [row(r - 1)[span, :], row(r)[span, :], row(r + 1)[span, :], sides[span, :]], axis=1
            )
            out = jnp.dot(lhs, split, preferred_element_type=f32)
            mean = ((out[:, :cols] + out[:, cols:]) * inverse).astype(jnp.bfloat16)
            a_ref[r, span, :] = mean
            mean32 = mean.astype(f32).reshape(CHUNK // 8, 8, cols)
            squares = squares + jnp.sum(mean32 * mean32, axis=0)
        energy = jnp.sum(squares, axis=0, keepdims=True) / pixels
        inv_ref[pl.ds(r, 1), :] = 1.0 / jnp.sqrt(energy + epsilon)


def average(block, left, right, dots, usable, *earlier):
    rows = block[2].shape[0] + 2
    pixels, cols = block[0].shape
    return pl.pallas_call(
        average_kernel,
        in_specs=[WHOLE] * (9 + len(earlier)),
        out_specs=(WHOLE, WHOLE),
        out_shape=(
            pltpu.VMEM((rows, pixels, cols), jnp.bfloat16),
            jax.ShapeDtypeStruct((rows, cols), jnp.float32),
        ),
        scratch_shapes=[
            pltpu.VMEM((pixels, cols), jnp.bfloat16),
            pltpu.VMEM((4, cols, cols), jnp.float32),
        ],
        compiler_params=pltpu.CompilerParams(vmem_limit_bytes=8 * MIB),
        cost_estimate=SHORT,
        name="average",
    )(*map(on_chip, block), left, right, dots, usable, *earlier)


def insert(best, new):
    kept = []
    for slot, held in enumerate(best):
        kept.append(jnp.maximum(held, new))
        if slot < len(best) - 1:
            new = jnp.minimum(held, new)
    return kept


def merge_sublanes(best):
    for shift in (4, 2, 1):
        other = [pltpu.roll(b, shift, 0) for b in best]
        m = [jnp.maximum(best[i], other[3 - i]) for i in range(4)]
        a, c = jnp.maximum(m[0], m[2]), jnp.minimum(m[0], m[2])
        b, d = jnp.maximum(m[1], m[3]), jnp.minimum(m[1], m[3])
        best = [jnp.maximum(a, b), jnp.minimum(a, b), jnp.maximum(c, d), jnp.minimum(c, d)]
    return best


def score_kernel(count, a_ref, best_ref, *refs):
    pieces, last = refs[:count], refs[count:]
    out = last[-1]
    rows, pixels, cols = a_ref.shape
    f32 = jnp.float32
    panels = pieces[0].shape[0]
    entries = jnp.concatenate([piece[k] for k in range(panels) for piece in pieces], axis=0)
    each = sum(piece.shape[1] for piece in pieces)
    entries32 = entries.astype(f32)
    energy = jnp.sum(entries32 * entries32, axis=1, keepdims=True) / pixels
    inv_entry = 1.0 / jnp.sqrt(energy + epsilon) / pixels
    for r in range(0, rows, 2):
        block = jnp.concatenate([a_ref[r], a_ref[r + 1]], axis=1)
        scores = jnp.dot(entries, block, preferred_element_type=f32) * inv_entry
        for k in range(panels):
            for half in range(2):
                held = [best_ref[k, j, r + half] for j in range(TOP)]
                for e in range(k * each, (k + 1) * each, 8):
                    held = insert(held, scores[e : e + 8, half * cols : (half + 1) * cols])
                if len(last) > 1:
                    inv = last[0][pl.ds(r + half, 1), :]
                    held = merge_sublanes(held)
                    for j in range(TOP):
                        out[k, j, pl.ds(r + half, 1), :] = held[j][:1] * inv
                else:
                    for j in range(TOP):
                        out[k, j, r + half] = held[j]


def score(averaged, best, pieces, inv_pattern=None):
    last = [] if inv_pattern is None else [inv_pattern]
    panels, top, rows, sublanes, cols = best.shape
    shape = (panels, top, rows, cols) if last else best.shape
    out = jax.ShapeDtypeStruct(shape, jnp.float32)
    return pl.pallas_call(
        functools.partial(score_kernel, len(pieces)),
        in_specs=[WHOLE] * (2 + len(pieces) + len(last)),
        out_specs=WHOLE,
        out_shape=out,
        compiler_params=pltpu.CompilerParams(vmem_limit_bytes=14 * MIB),
        cost_estimate=SHORT,
        name="score",
    )(on_chip(averaged), best, *pieces, *last)


def exchange(x, axis, masks):
    count = lax.axis_size(axis)
    return lax.ppermute(x, axis, [(i, i ^ masks[i & 1]) for i in range(count)])


def power_of_two(n):
    return n & (n - 1) == 0


def hold(x, *earlier):
    def nothing(*refs):
        pass

    return pl.pallas_call(
        nothing,
        in_specs=[APART] + [WHOLE] * len(earlier),
        out_specs=APART,
        out_shape=jax.ShapeDtypeStruct(x.shape, x.dtype),
        input_output_aliases={0: 0},
        compiler_params=pltpu.CompilerParams(vmem_limit_bytes=MIB),
        cost_estimate=SHORT,
        name="hold",
    )(x, *earlier)


def join_kernel(count, *refs):
    parts, (out, token, sems) = refs[:count], refs[-3:]
    mark(token)
    copies, at = [], 0
    for i, part in enumerate(parts):
        size = part.shape[1]
        copies.append(pltpu.make_async_copy(part, out.at[:, pl.ds(at, size)], sems.at[i]))
        at += size
    for copy in copies:
        copy.start()
    for copy in copies:
        copy.wait()


def join(parts, *earlier):
    panels, _, pixels = parts[0].shape
    if any(part.shape[1] % 16 for part in parts):
        whole = jnp.concatenate(parts, axis=1)
        return hold(whole, *earlier), jnp.zeros(TOKEN.shape, TOKEN.dtype)
    size = sum(part.shape[1] for part in parts)
    return pl.pallas_call(
        functools.partial(join_kernel, len(parts)),
        in_specs=[APART] * len(parts) + [WHOLE] * len(earlier),
        out_specs=(APART, WHOLE),
        out_shape=(jax.ShapeDtypeStruct((panels, size, pixels), parts[0].dtype), TOKEN),
        scratch_shapes=[pltpu.SemaphoreType.DMA((len(parts),))],
        compiler_params=pltpu.CompilerParams(vmem_limit_bytes=MIB),
        cost_estimate=SHORT,
        name="join",
    )(*parts, *earlier)


def gathers(strip, line):
    return power_of_two(strip) and power_of_two(line) and strip > 2 and line > 1


def strip_masks(strip):
    bits = [1 << i for i in range(1, strip.bit_length() - 1)]
    return list(zip(bits, reversed(bits)))


def from_low(x, axis):
    count = lax.axis_size(axis)
    return lax.ppermute(x, axis, [(i, i + 1) for i in range(count - 1)])


def from_high(x, axis):
    count = lax.axis_size(axis)
    return lax.ppermute(x, axis, [(i + 1, i) for i in range(count - 1)])


def usable_neighbours(neighbour_mask):
    _, rows, cols = neighbour_mask.shape
    row_at = lax.axis_index("strip") * rows + jnp.arange(rows, dtype=jnp.int32)
    col_at = lax.axis_index("dict") * cols + jnp.arange(cols, dtype=jnp.int32)
    all_rows = rows * lax.axis_size("strip")
    all_cols = cols * lax.axis_size("dict")
    inside = []
    for dr in (-1, 0, 1):
        for dc in (-1, 0, 1):
            if dr == 0 and dc == 0:
                continue
            row_ok = (row_at + dr >= 0) & (row_at + dr < all_rows)
            col_ok = (col_at + dc >= 0) & (col_at + dc < all_cols)
            inside.append(row_ok[:, None] & col_ok[None, :])
    return (jnp.stack(inside) & (neighbour_mask == 1)).astype(jnp.float32)


def on_device(patterns, scan_mask, neighbour_mask, dictionary):
    rows, cols = scan_mask.shape
    strip, line = lax.axis_size("strip"), lax.axis_size("dict")
    alone = not gathers(strip, line)
    matrices = jnp.asarray(pass_matrices())
    usable = usable_neighbours(neighbour_mask)
    best = jnp.full((dictionary.shape[0], TOP, rows, 8, cols), -jnp.inf, jnp.float32)
    if not alone:
        ways = strip_masks(strip)
        near = dictionary
        near_new = exchange(near, "strip", ways[0])
        far = [exchange(dictionary, "dict", (mask, mask)) for mask in range(1, line)]

    xq, first, last, bordered = border(patterns, scan_mask, matrices)
    above = from_low(last, "strip")
    below = from_high(first, "strip")
    done = bordered
    if not alone:
        for way in ways[1:]:
            near, done = join([near, near_new], bordered)
            near_new = exchange(near, "strip", way)

    middle, filled = interior(xq, matrices, done)
    block = (above, first, middle, last, below)
    joined = [filled]
    if not alone:
        near, done = join([near, near_new], filled)
        near_other = exchange(near, "strip", (1, 1))
        far, done = join(far, done)
        far_new = exchange(far, "strip", ways[0])
        joined = [done]

    own_left, own_right, dots = products(block, *joined)
    left = from_low(own_right, "dict")
    right = from_high(own_left, "dict")
    joined = []
    if not alone:
        for way in ways[1:]:
            far, done = join([far, far_new], dots)
            far_new = exchange(far, "strip", way)
        joined = [done]
        far_other = exchange(far, "strip", (1, 1))

    averaged, inv_pattern = average(block, left, right, dots, usable, *joined)
    if alone:
        whole = lax.all_gather(dictionary, ("strip", "dict"), axis=1, tiled=True)
        return score(averaged, best, [whole], inv_pattern)
    best = score(averaged, best, [near, near_other])
    far_new = hold(far_new, best)
    far_new_other = exchange(far_new, "strip", (1, 1))
    best = score(averaged, best, [far, far_other])
    best = score(averaged, best, [far_new])
    return score(averaged, best, [far_new_other], inv_pattern)


def solution(mesh):
    in_specs = (
        P(None, "strip", "dict"),
        P("strip", "dict"),
        P(None, "strip", "dict"),
        P(None, ("strip", "dict"), None),
    )
    out_specs = P(None, None, "strip", "dict")
    return jax.shard_map(
        on_device, mesh=mesh, in_specs=in_specs, out_specs=out_specs, check_vma=False
    )
```

```python
import functools

import jax
import jax.numpy as jnp
import ml_dtypes
import numpy as np
from jax import lax
from jax.experimental import pallas as pl
from jax.experimental.pallas import tpu as pltpu
from jax.sharding import PartitionSpec as P

PH = 60
TOP = 4
QUAD = 4
GROUPS = PH // QUAD
TILE = QUAD * QUAD
CHUNK = GROUPS * TILE
DEPTH = 256
LANES = 128
SIDES = 32

epsilon = 1e-05
nlpar_scale = 2.0
MIB = 1 << 20


def blur_matrix():
    at = np.arange(PH, dtype=np.float32)
    spread_px = np.float32(PH / 8.0)
    gap = at[:, None] - at[None, :]
    profile = np.exp(-(gap * gap) / (np.float32(2.0) * spread_px * spread_px))
    profile = profile / profile.sum(axis=1, keepdims=True)
    return profile.astype(ml_dtypes.bfloat16).astype(np.float32)


def pass_matrices():
    kernel = blur_matrix()
    index = np.arange(CHUNK)
    quad, row, col = index // TILE, (index // QUAD) % QUAD, index % QUAD
    along = quad * QUAD + col
    columns = kernel[along[:, None], along[None, :]] * (row[:, None] == row[None, :])
    down = quad * QUAD + row
    rows = kernel[down[:, None], down[None, :]] * (col[:, None] == col[None, :])
    natural = row * PH + along
    order = (index[:, None] == natural[None, :]).astype(np.float32)
    out = np.zeros((3, CHUNK, DEPTH), np.float32)
    out[0, :, :CHUNK], out[1, :, :CHUNK], out[2, :, :CHUNK] = columns, rows, order
    return out.astype(ml_dtypes.bfloat16)


def tiles_of(pieces):
    return jnp.concatenate(pieces + [pieces[-1]], axis=0)


def on_chip(x):
    return pltpu.with_memory_space_constraint(x, pltpu.VMEM)


def in_hbm(x):
    return pltpu.with_memory_space_constraint(x, pltpu.HBM)


WHOLE = pl.BlockSpec(memory_space=pltpu.VMEM)
APART = pl.BlockSpec(memory_space=pl.ANY)
SHORT = pl.CostEstimate(flops=1000, bytes_accessed=1000, transcendentals=0)
TOKEN = jax.ShapeDtypeStruct((8, LANES), jnp.float32)


def mark(ref):
    ref[...] = jnp.zeros(ref.shape, ref.dtype)


def standard_rows(both, mat_ref, half, corr, sq, stores):
    for g in range(GROUPS):
        rhs = tiles_of([both(quad, slice(g * TILE, (g + 1) * TILE)) for quad in range(GROUPS)])
        out = jnp.dot(mat_ref[0], rhs, preferred_element_type=jnp.float32)
        half[g] = out.astype(jnp.bfloat16)

    total = jnp.zeros((8, 2 * LANES), jnp.float32)
    squares = jnp.zeros((8, 2 * LANES), jnp.float32)
    for quad in range(GROUPS):
        rhs = tiles_of([half[g, pl.ds(quad * TILE, TILE), :] for g in range(GROUPS)])
        background = jnp.dot(mat_ref[1], rhs, preferred_element_type=jnp.float32)
        corrected = both(quad, slice(None)).astype(jnp.float32) - background
        corr[quad] = corrected
        folded = corrected.reshape(CHUNK // 8, 8, 2 * LANES)
        total = total + jnp.sum(folded, axis=0)
        squares = squares + jnp.sum(folded * folded, axis=0)
    pixels = GROUPS * CHUNK
    mean = jnp.sum(total, axis=0, keepdims=True) / pixels
    variance = jnp.sum(squares, axis=0, keepdims=True) / pixels - mean * mean
    scale = 1.0 / jnp.sqrt(jnp.maximum(variance, 0.0) + epsilon)
    for quad in range(GROUPS):
        sq[quad] = ((corr[quad] - mean) * scale).astype(jnp.bfloat16)
    for g in range(GROUPS):
        rhs = tiles_of([sq[quad, pl.ds(g * TILE, TILE), :] for quad in range(GROUPS)])
        out = jnp.dot(mat_ref[2], rhs, preferred_element_type=jnp.float32).astype(jnp.bfloat16)
        for side, store in enumerate(stores):
            store(slice(g * CHUNK, (g + 1) * CHUNK), out[:, side * LANES : (side + 1) * LANES])


def border_kernel(x_hbm, mask_hbm, mat_hbm, xq_hbm, first, last, token, mask_ref, mat_ref, xq, ends, raw, half, corr, sq, sems):
    rows = raw.shape[2]
    mark(token)

    def fetch(g):
        return pltpu.make_async_copy(x_hbm.at[pl.ds(g * CHUNK, CHUNK)], raw.at[g], sems.at[g])

    mask_copy = pltpu.make_async_copy(mask_hbm, mask_ref, sems.at[GROUPS])
    matrices = pltpu.make_async_copy(mat_hbm, mat_ref, sems.at[GROUPS + 1])
    keep = pltpu.make_async_copy(xq, xq_hbm, sems.at[GROUPS + 2])
    mask_copy.start()
    for g in range(GROUPS):
        fetch(g).start()
    matrices.start()
    mask_copy.wait()
    mask = mask_ref[...].astype(jnp.bfloat16)[None]
    for g in range(GROUPS):
        fetch(g).wait()
        for quad in range(GROUPS):
            piece = jnp.concatenate(
                [raw[g, pl.ds(row * PH + quad * QUAD, QUAD)] for row in range(QUAD)], axis=0
            )
            tile = jnp.swapaxes(piece * mask, 0, 1)
            span = slice(g * TILE, (g + 1) * TILE)
            xq[:, quad, span, :] = tile[1 : rows - 1]
            ends[0, quad, span, :] = tile[0]
            ends[1, quad, span, :] = tile[rows - 1]
    keep.start()
    matrices.wait()

    def both(quad, span):
        return jnp.concatenate([ends[0, quad, span, :], ends[1, quad, span, :]], axis=1)

    def store(ref):
        def put(span, value):
            ref[span, :] = value

        return put

    standard_rows(both, mat_ref, half, corr, sq, [store(first), store(last)])
    keep.wait()


def row_scratch(cols):
    return [
        pltpu.VMEM((GROUPS, CHUNK, 2 * cols), jnp.bfloat16),
        pltpu.VMEM((GROUPS, CHUNK, 2 * cols), jnp.float32),
        pltpu.VMEM((GROUPS, CHUNK, 2 * cols), jnp.bfloat16),
    ]


def border(patterns, scan_mask, matrices):
    pixels, rows, cols = patterns.shape
    bf16 = jnp.bfloat16
    return pl.pallas_call(
        border_kernel,
        in_specs=[APART] * 3,
        out_specs=(APART, WHOLE, WHOLE, WHOLE),
        out_shape=(
            pltpu.HBM((rows - 2, GROUPS, CHUNK, cols), bf16),
            pltpu.VMEM((pixels, cols), bf16),
            pltpu.VMEM((pixels, cols), bf16),
            TOKEN,
        ),
        scratch_shapes=[
            pltpu.VMEM((rows, cols), scan_mask.dtype),
            pltpu.VMEM(matrices.shape, bf16),
            pltpu.VMEM((rows - 2, GROUPS, CHUNK, cols), bf16),
            pltpu.VMEM((2, GROUPS, CHUNK, cols), bf16),
            pltpu.VMEM((GROUPS, CHUNK, rows, cols), bf16),
        ]
        + row_scratch(cols)
        + [pltpu.SemaphoreType.DMA((GROUPS + 3,))],
        compiler_params=pltpu.CompilerParams(vmem_limit_bytes=26 * MIB),
        cost_estimate=SHORT,
        name="border",
    )(in_hbm(patterns), in_hbm(scan_mask), in_hbm(matrices))


def interior_kernel(xq_hbm, mat_hbm, *refs):
    s_ref, token, mat_ref, xq, half, corr, sq, sems = refs[-8:]
    mark(token)
    pairs = s_ref.shape[0] // 2
    matrices = pltpu.make_async_copy(mat_hbm, mat_ref, sems.at[2])

    def fetch(i):
        slot = i % 2
        return pltpu.make_async_copy(xq_hbm.at[pl.ds(2 * i, 2)], xq.at[slot], sems.at[slot])

    fetch(0).start()
    matrices.start()
    if pairs > 1:
        fetch(1).start()
    matrices.wait()

    def work(source, at):
        def both(quad, span):
            return jnp.concatenate([source[0, quad, span, :], source[1, quad, span, :]], axis=1)

        def store(side):
            def put(span, value):
                s_ref[at + side, span, :] = value

            return put

        standard_rows(both, mat_ref, half, corr, sq, [store(0), store(1)])

    for i in range(pairs):
        fetch(i).wait()
        work(xq.at[i % 2], 2 * i)
        if i + 2 < pairs:
            fetch(i + 2).start()


def interior(xq, matrices, *earlier):
    rows, _, _, cols = xq.shape
    pixels = GROUPS * CHUNK
    return pl.pallas_call(
        interior_kernel,
        in_specs=[APART, APART] + [WHOLE] * len(earlier),
        out_specs=(WHOLE, WHOLE),
        out_shape=(pltpu.VMEM((rows, pixels, cols), jnp.bfloat16), TOKEN),
        scratch_shapes=[
            pltpu.VMEM(matrices.shape, jnp.bfloat16),
            pltpu.VMEM((2, 2, GROUPS, CHUNK, cols), jnp.bfloat16),
        ]
        + row_scratch(cols)
        + [pltpu.SemaphoreType.DMA((3,))],
        compiler_params=pltpu.CompilerParams(vmem_limit_bytes=16 * MIB),
        cost_estimate=SHORT,
        name="interior",
    )(in_hbm(xq), in_hbm(matrices), *earlier)


def row_of(refs, rows):
    above, first, middle, last, below = refs

    def row(r):
        if 1 <= r < rows - 1:
            return middle.at[r - 1]
        return {-1: above, 0: first, rows - 1: last, rows: below}[r]

    return row


def diagonals(product, at_sub, at_lane):
    return [
        jnp.sum(jnp.where(at_sub == at_lane + d, product, 0.0), axis=0, keepdims=True)
        for d in (-1, 0, 1)
    ]


PER_ROW = 8


def products_kernel(*refs):
    left, right, out = refs[-3:]
    rows = refs[2].shape[0] + 2
    row = row_of(refs[:5], rows)
    cols = refs[0].shape[1]
    f32 = jnp.float32
    at_sub = lax.broadcasted_iota(jnp.int32, (cols, cols), 0)
    at_lane = lax.broadcasted_iota(jnp.int32, (cols, cols), 1)
    firsts, lasts = [], []
    for r in range(-1, rows + 1):
        here = row(r)[...]
        across = here.T
        firsts.append(across[:1])
        lasts.append(across[cols - 1 :])
        pieces = [here]
        if r < rows:
            pieces.append(row(r + 1)[...])
        product = jnp.dot(across, jnp.concatenate(pieces, axis=1), preferred_element_type=f32)
        own = diagonals(product[:, :cols], at_sub, at_lane)
        vectors = [own[1], own[0]]
        if r < rows:
            vectors += diagonals(product[:, cols:], at_sub, at_lane)
        vectors += [jnp.zeros((1, cols), f32)] * (PER_ROW - len(vectors))
        out[r + 1] = jnp.concatenate(vectors, axis=0)
    blank = [jnp.zeros((SIDES // 2 - len(firsts), here.shape[0]), firsts[0].dtype)]
    left[...] = jnp.concatenate(firsts + blank, axis=0)
    right[...] = jnp.concatenate(lasts + blank, axis=0)


def products(block, *earlier):
    rows = block[2].shape[0] + 2
    pixels, cols = block[0].shape
    one = jax.ShapeDtypeStruct((SIDES // 2, pixels), jnp.bfloat16)
    return pl.pallas_call(
        products_kernel,
        in_specs=[WHOLE] * (5 + len(earlier)),
        out_specs=(WHOLE,) * 3,
        out_shape=(one, one, jax.ShapeDtypeStruct((rows + 2, PER_ROW, cols), jnp.float32)),
        compiler_params=pltpu.CompilerParams(vmem_limit_bytes=12 * MIB),
        cost_estimate=SHORT,
        name="products",
    )(*map(on_chip, block), *earlier)


def average_kernel(*refs):
    left_ref, right_ref, own_left_ref, own_right_ref, dot_ref, usable_ref = refs[5:11]
    a_ref, inv_ref, sides, weights = refs[-4:]
    rows, pixels, cols = a_ref.shape
    row = row_of(refs[:5], rows)
    f32 = jnp.float32
    at_sub = lax.broadcasted_iota(jnp.int32, (cols, cols), 0)
    at_lane = lax.broadcasted_iota(jnp.int32, (cols, cols), 1)
    lane = lax.broadcasted_iota(jnp.int32, (1, cols), 1)

    pad = jnp.zeros((LANES, cols - SIDES), f32)
    for start in range(0, pixels, LANES):
        width = min(LANES, pixels - start)
        span = slice(start, start + width)
        piece = jnp.concatenate([left_ref[:, span], right_ref[:, span]], axis=0).astype(f32)
        sides[span, :] = jnp.concatenate([piece.T, pad[:width]], axis=1).astype(jnp.bfloat16)

    meet = []
    for own, halo in ((own_left_ref, left_ref), (own_right_ref, right_ref)):
        both = jnp.concatenate([own[...], halo[...]], axis=0)
        meet.append(
            lax.dot_general(both, halo[...], (((1,), (1,)), ((), ())), preferred_element_type=f32)
        )

    def shifted(vector, dc):
        if dc == 0:
            return vector
        return pltpu.roll(vector, (-dc) % cols, 1)

    def kept(r, k):
        return dot_ref[r + 1, pl.ds(k, 1), :]

    for r in range(rows):
        weight = {}
        slot = 0
        total = jnp.ones((1, cols), f32)
        for dr in (-1, 0, 1):
            for dc in (-1, 0, 1):
                if dr == 0 and dc == 0:
                    continue
                if dr == -1:
                    dot = kept(r - 1, 3 + dc)
                elif dr == 1:
                    dot = shifted(kept(r, 3 - dc), dc)
                else:
                    dot = kept(r, 1) if dc == -1 else shifted(kept(r, 1), 1)
                other = shifted(kept(r + dr, 0), dc)
                if dc != 0:
                    k, near = r + dr + 1, meet[0 if dc < 0 else 1]
                    end = 0 if dc < 0 else cols - 1
                    half = SIDES // 2
                    dot = jnp.where(lane == end, near[r + 1 : r + 2, k : k + 1], dot)
                    other = jnp.where(lane == end, near[half + k : half + k + 1, k : k + 1], other)
                distance = jnp.maximum(kept(r, 0) + other - 2.0 * dot, 0.0) / pixels
                weight[dr, dc] = usable_ref[slot, pl.ds(r, 1), :] * jnp.exp(-distance / nlpar_scale)
                total = total + weight[dr, dc]
                slot += 1
        for dr in (-1, 0, 1):
            block = jnp.zeros((cols, cols), f32)
            for dc in (-1, 0, 1):
                w = jnp.ones((1, cols), f32) if dr == 0 and dc == 0 else weight[dr, dc]
                block = jnp.where(at_sub == at_lane + dc, w, block)
            weights[dr + 1] = block
        block = jnp.zeros((cols, cols), f32)
        for dr in (-1, 0, 1):
            for dc in (-1, 1):
                k = r + dr + 1 + (0 if dc < 0 else 16)
                end = 0 if dc < 0 else cols - 1
                block = jnp.where((at_sub == k) & (at_lane == end), weight[dr, dc], block)
        weights[3] = block

        full = weights[...].reshape(4 * cols, cols)
        high = full.astype(jnp.bfloat16)
        low = (full - high.astype(f32)).astype(jnp.bfloat16)
        split = jnp.concatenate([high, low], axis=1)
        inverse = 1.0 / total
        squares = jnp.zeros((8, cols), f32)
        for g in range(GROUPS):
            span = slice(g * CHUNK, (g + 1) * CHUNK)
            lhs = jnp.concatenate(
                [row(r - 1)[span, :], row(r)[span, :], row(r + 1)[span, :], sides[span, :]], axis=1
            )
            out = jnp.dot(lhs, split, preferred_element_type=f32)
            mean = ((out[:, :cols] + out[:, cols:]) * inverse).astype(jnp.bfloat16)
            a_ref[r, span, :] = mean
            mean32 = mean.astype(f32).reshape(CHUNK // 8, 8, cols)
            squares = squares + jnp.sum(mean32 * mean32, axis=0)
        energy = jnp.sum(squares, axis=0, keepdims=True) / pixels
        inv_ref[pl.ds(r, 1), :] = 1.0 / jnp.sqrt(energy + epsilon)


def average(block, left, right, own_left, own_right, dots, usable, *earlier):
    rows = block[2].shape[0] + 2
    pixels, cols = block[0].shape
    return pl.pallas_call(
        average_kernel,
        in_specs=[WHOLE] * (11 + len(earlier)),
        out_specs=(WHOLE, WHOLE),
        out_shape=(
            pltpu.VMEM((rows, pixels, cols), jnp.bfloat16),
            jax.ShapeDtypeStruct((rows, cols), jnp.float32),
        ),
        scratch_shapes=[
            pltpu.VMEM((pixels, cols), jnp.bfloat16),
            pltpu.VMEM((4, cols, cols), jnp.float32),
        ],
        compiler_params=pltpu.CompilerParams(vmem_limit_bytes=8 * MIB),
        cost_estimate=SHORT,
        name="average",
    )(*map(on_chip, block), left, right, own_left, own_right, dots, usable, *earlier)


def insert(best, new):
    kept = []
    for slot, held in enumerate(best):
        kept.append(jnp.maximum(held, new))
        if slot < len(best) - 1:
            new = jnp.minimum(held, new)
    return kept


def merge_sublanes(best):
    for shift in (4, 2, 1):
        other = [pltpu.roll(b, shift, 0) for b in best]
        m = [jnp.maximum(best[i], other[3 - i]) for i in range(4)]
        a, c = jnp.maximum(m[0], m[2]), jnp.minimum(m[0], m[2])
        b, d = jnp.maximum(m[1], m[3]), jnp.minimum(m[1], m[3])
        best = [jnp.maximum(a, b), jnp.minimum(a, b), jnp.maximum(c, d), jnp.minimum(c, d)]
    return best


def score_kernel(count, a_ref, best_ref, *refs):
    pieces, last = refs[:count], refs[count:]
    out = last[-1]
    rows, pixels, cols = a_ref.shape
    f32 = jnp.float32
    panels = pieces[0].shape[0]
    entries = jnp.concatenate([piece[k] for k in range(panels) for piece in pieces], axis=0)
    each = sum(piece.shape[1] for piece in pieces)
    entries32 = entries.astype(f32)
    energy = jnp.sum(entries32 * entries32, axis=1, keepdims=True) / pixels
    inv_entry = 1.0 / jnp.sqrt(energy + epsilon) / pixels
    for r in range(0, rows, 2):
        block = jnp.concatenate([a_ref[r], a_ref[r + 1]], axis=1)
        scores = jnp.dot(entries, block, preferred_element_type=f32) * inv_entry
        for k in range(panels):
            for half in range(2):
                held = [best_ref[k, j, r + half] for j in range(TOP)]
                for e in range(k * each, (k + 1) * each, 8):
                    held = insert(held, scores[e : e + 8, half * cols : (half + 1) * cols])
                if len(last) > 1:
                    inv = last[0][pl.ds(r + half, 1), :]
                    held = merge_sublanes(held)
                    for j in range(TOP):
                        out[k, j, pl.ds(r + half, 1), :] = held[j][:1] * inv
                else:
                    for j in range(TOP):
                        out[k, j, r + half] = held[j]


def score(averaged, best, pieces, inv_pattern=None):
    last = [] if inv_pattern is None else [inv_pattern]
    panels, top, rows, sublanes, cols = best.shape
    shape = (panels, top, rows, cols) if last else best.shape
    out = jax.ShapeDtypeStruct(shape, jnp.float32)
    return pl.pallas_call(
        functools.partial(score_kernel, len(pieces)),
        in_specs=[WHOLE] * (2 + len(pieces) + len(last)),
        out_specs=WHOLE,
        out_shape=out,
        compiler_params=pltpu.CompilerParams(vmem_limit_bytes=14 * MIB),
        cost_estimate=SHORT,
        name="score",
    )(on_chip(averaged), best, *pieces, *last)


def exchange(x, axis, masks):
    count = lax.axis_size(axis)
    return lax.ppermute(x, axis, [(i, i ^ masks[i & 1]) for i in range(count)])


def power_of_two(n):
    return n & (n - 1) == 0


def hold(x, *earlier):
    def nothing(*refs):
        pass

    return pl.pallas_call(
        nothing,
        in_specs=[APART] + [WHOLE] * len(earlier),
        out_specs=APART,
        out_shape=jax.ShapeDtypeStruct(x.shape, x.dtype),
        input_output_aliases={0: 0},
        compiler_params=pltpu.CompilerParams(vmem_limit_bytes=MIB),
        cost_estimate=SHORT,
        name="hold",
    )(x, *earlier)


def join_kernel(count, *refs):
    parts, (out, token, sems) = refs[:count], refs[-3:]
    mark(token)
    copies, at = [], 0
    for i, part in enumerate(parts):
        size = part.shape[1]
        copies.append(pltpu.make_async_copy(part, out.at[:, pl.ds(at, size)], sems.at[i]))
        at += size
    for copy in copies:
        copy.start()
    for copy in copies:
        copy.wait()


def join(parts, *earlier):
    panels, _, pixels = parts[0].shape
    if any(part.shape[1] % 16 for part in parts):
        whole = jnp.concatenate(parts, axis=1)
        return hold(whole, *earlier), jnp.zeros(TOKEN.shape, TOKEN.dtype)
    size = sum(part.shape[1] for part in parts)
    return pl.pallas_call(
        functools.partial(join_kernel, len(parts)),
        in_specs=[APART] * len(parts) + [WHOLE] * len(earlier),
        out_specs=(APART, WHOLE),
        out_shape=(jax.ShapeDtypeStruct((panels, size, pixels), parts[0].dtype), TOKEN),
        scratch_shapes=[pltpu.SemaphoreType.DMA((len(parts),))],
        compiler_params=pltpu.CompilerParams(vmem_limit_bytes=MIB),
        cost_estimate=SHORT,
        name="join",
    )(*parts, *earlier)


def gathers(strip, line):
    return power_of_two(strip) and power_of_two(line) and strip > 2 and line > 1


def line_masks(line):
    return [line - 1] + [1 << i for i in range(line.bit_length() - 2)]


def strip_masks(strip):
    bits = [1 << i for i in range(1, strip.bit_length() - 1)]
    return list(zip(bits, reversed(bits)))


def from_low(x, axis):
    count = lax.axis_size(axis)
    return lax.ppermute(x, axis, [(i, i + 1) for i in range(count - 1)])


def from_high(x, axis):
    count = lax.axis_size(axis)
    return lax.ppermute(x, axis, [(i + 1, i) for i in range(count - 1)])


def usable_neighbours(neighbour_mask):
    _, rows, cols = neighbour_mask.shape
    row_at = lax.axis_index("strip") * rows + jnp.arange(rows, dtype=jnp.int32)
    col_at = lax.axis_index("dict") * cols + jnp.arange(cols, dtype=jnp.int32)
    all_rows = rows * lax.axis_size("strip")
    all_cols = cols * lax.axis_size("dict")
    inside = []
    for dr in (-1, 0, 1):
        for dc in (-1, 0, 1):
            if dr == 0 and dc == 0:
                continue
            row_ok = (row_at + dr >= 0) & (row_at + dr < all_rows)
            col_ok = (col_at + dc >= 0) & (col_at + dc < all_cols)
            inside.append(row_ok[:, None] & col_ok[None, :])
    return (jnp.stack(inside) & (neighbour_mask == 1)).astype(jnp.float32)


def on_device(patterns, scan_mask, neighbour_mask, dictionary):
    rows, cols = scan_mask.shape
    strip, line = lax.axis_size("strip"), lax.axis_size("dict")
    alone = not gathers(strip, line)
    matrices = jnp.asarray(pass_matrices())
    usable = usable_neighbours(neighbour_mask)
    best = jnp.full((dictionary.shape[0], TOP, rows, 8, cols), -jnp.inf, jnp.float32)
    if not alone:
        ways = strip_masks(strip)
        near = held = dictionary
        mirrored, *masks = line_masks(line)
        far = [exchange(held, "dict", (mirrored, mirrored))]
        plain = [(even, even) for even, _ in ways]
        near_new = exchange(near, "strip", plain[0])

    xq, first, last, bordered = border(patterns, scan_mask, matrices)
    above = from_low(last, "strip")
    below = from_high(first, "strip")
    joined = [bordered]
    if not alone:
        for mask in masks:
            held, done = join([held, far[-1]], bordered)
            far.append(exchange(held, "dict", (mask, mask)))
            joined.append(done)
        for way in plain[1:]:
            near, done = join([near, near_new], bordered)
            near_new = exchange(near, "strip", way)
            joined.append(done)

    middle, filled = interior(xq, matrices, *joined)
    block = (above, first, middle, last, below)
    joined = [filled]
    if not alone:
        near, done = join([near, near_new], filled)
        near_other = exchange(near, "strip", (1, 1))
        far, done = join(far, done)
        far_new = exchange(far, "strip", ways[0])
        joined = [done]

    own_left, own_right, dots = products(block, *joined)
    left = from_low(own_right, "dict")
    right = from_high(own_left, "dict")
    joined = []
    if not alone:
        for way in ways[1:]:
            far, done = join([far, far_new], left, right)
            far_new = exchange(far, "strip", way)
        joined = [done]
        far_other = exchange(far, "strip", (1, 1))

    averaged, inv_pattern = average(block, left, right, own_left, own_right, dots, usable, *joined)
    if alone:
        whole = lax.all_gather(dictionary, ("strip", "dict"), axis=1, tiled=True)
        return score(averaged, best, [whole], inv_pattern)
    best = score(averaged, best, [near, near_other])
    best = score(averaged, best, [far, far_other])
    far_new = hold(far_new, best)
    far_new_other = exchange(far_new, "strip", (1, 1))
    best = score(averaged, best, [far_new])
    return score(averaged, best, [far_new_other], inv_pattern)


def solution(mesh):
    in_specs = (
        P(None, "strip", "dict"),
        P("strip", "dict"),
        P(None, "strip", "dict"),
        P(None, ("strip", "dict"), None),
    )
    out_specs = P(None, None, "strip", "dict")
    return jax.shard_map(
        on_device, mesh=mesh, in_specs=in_specs, out_specs=out_specs, check_vma=False
    )
```

```python
import functools

import jax
import jax.numpy as jnp
import ml_dtypes
import numpy as np
from jax import lax
from jax.experimental import pallas as pl
from jax.experimental.pallas import tpu as pltpu
from jax.sharding import PartitionSpec as P

PH = 60
TOP = 4
QUAD = 4
GROUPS = PH // QUAD
TILE = QUAD * QUAD
CHUNK = GROUPS * TILE
DEPTH = 256
LANES = 128
SLOTS = 6
SIDES = 32

epsilon = 1e-05
nlpar_scale = 2.0
MIB = 1 << 20


def blur_matrix():
    at = np.arange(PH, dtype=np.float32)
    spread_px = np.float32(PH / 8.0)
    gap = at[:, None] - at[None, :]
    profile = np.exp(-(gap * gap) / (np.float32(2.0) * spread_px * spread_px))
    profile = profile / profile.sum(axis=1, keepdims=True)
    return profile.astype(ml_dtypes.bfloat16).astype(np.float32)


def pass_matrices():
    kernel = blur_matrix()
    index = np.arange(CHUNK)
    quad, row, col = index // TILE, (index // QUAD) % QUAD, index % QUAD
    along = quad * QUAD + col
    columns = kernel[along[:, None], along[None, :]] * (row[:, None] == row[None, :])
    down = quad * QUAD + row
    rows = kernel[down[:, None], down[None, :]] * (col[:, None] == col[None, :])
    natural = row * PH + along
    order = (index[:, None] == natural[None, :]).astype(np.float32)
    out = np.zeros((3, CHUNK, DEPTH), np.float32)
    out[0, :, :CHUNK], out[1, :, :CHUNK], out[2, :, :CHUNK] = columns, rows, order
    return out.astype(ml_dtypes.bfloat16)


def tiles_of(pieces):
    return jnp.concatenate(pieces + [pieces[-1]], axis=0)


def on_chip(x):
    return pltpu.with_memory_space_constraint(x, pltpu.VMEM)


def in_hbm(x):
    return pltpu.with_memory_space_constraint(x, pltpu.HBM)


WHOLE = pl.BlockSpec(memory_space=pltpu.VMEM)
APART = pl.BlockSpec(memory_space=pl.ANY)
SHORT = pl.CostEstimate(flops=1000, bytes_accessed=1000, transcendentals=0)
TOKEN = jax.ShapeDtypeStruct((8, LANES), jnp.float32)


def mark(ref):
    ref[...] = jnp.zeros(ref.shape, ref.dtype)


def standard_rows(both, mat_ref, work, corr, stores):
    for g in range(GROUPS):
        rhs = tiles_of([both(quad, slice(g * TILE, (g + 1) * TILE)) for quad in range(GROUPS)])
        out = jnp.dot(mat_ref[0], rhs, preferred_element_type=jnp.float32)
        work[g] = out.astype(jnp.bfloat16)

    total = jnp.zeros((8, 2 * LANES), jnp.float32)
    squares = jnp.zeros((8, 2 * LANES), jnp.float32)
    for quad in range(GROUPS):
        rhs = tiles_of([work[g, pl.ds(quad * TILE, TILE), :] for g in range(GROUPS)])
        background = jnp.dot(mat_ref[1], rhs, preferred_element_type=jnp.float32)
        corrected = both(quad, slice(None)).astype(jnp.float32) - background
        corr[quad] = corrected
        folded = corrected.reshape(CHUNK // 8, 8, 2 * LANES)
        total = total + jnp.sum(folded, axis=0)
        squares = squares + jnp.sum(folded * folded, axis=0)
    pixels = GROUPS * CHUNK
    mean = jnp.sum(total, axis=0, keepdims=True) / pixels
    variance = jnp.sum(squares, axis=0, keepdims=True) / pixels - mean * mean
    scale = 1.0 / jnp.sqrt(jnp.maximum(variance, 0.0) + epsilon)
    for quad in range(GROUPS):
        work[quad] = ((corr[quad] - mean) * scale).astype(jnp.bfloat16)
    for g in range(GROUPS):
        rhs = tiles_of([work[quad, pl.ds(g * TILE, TILE), :] for quad in range(GROUPS)])
        out = jnp.dot(mat_ref[2], rhs, preferred_element_type=jnp.float32).astype(jnp.bfloat16)
        for side, store in enumerate(stores):
            store(slice(g * CHUNK, (g + 1) * CHUNK), out[:, side * LANES : (side + 1) * LANES])


def border_kernel(x_hbm, mask_hbm, mat_hbm, xq_hbm, first, last, token, mask_ref, mat_ref, xq, ends, raw, work, corr, sems):
    rows, slots = raw.shape[2], raw.shape[0]
    mark(token)

    def fetch(g):
        slot = g % slots
        return pltpu.make_async_copy(x_hbm.at[pl.ds(g * CHUNK, CHUNK)], raw.at[slot], sems.at[slot])

    mask_copy = pltpu.make_async_copy(mask_hbm, mask_ref, sems.at[slots])
    matrices = pltpu.make_async_copy(mat_hbm, mat_ref, sems.at[slots + 1])
    keep = pltpu.make_async_copy(xq, xq_hbm, sems.at[slots + 2])
    mask_copy.start()
    for g in range(slots):
        fetch(g).start()
    matrices.start()
    mask_copy.wait()
    mask = mask_ref[...].astype(jnp.bfloat16)[None]
    for g in range(GROUPS):
        fetch(g).wait()
        for quad in range(GROUPS):
            piece = jnp.concatenate(
                [raw[g % slots, pl.ds(row * PH + quad * QUAD, QUAD)] for row in range(QUAD)], axis=0
            )
            tile = jnp.swapaxes(piece * mask, 0, 1)
            span = slice(g * TILE, (g + 1) * TILE)
            xq[:, quad, span, :] = tile[1 : rows - 1]
            ends[0, quad, span, :] = tile[0]
            ends[1, quad, span, :] = tile[rows - 1]
        if g + slots < GROUPS:
            fetch(g + slots).start()
    keep.start()
    matrices.wait()

    def both(quad, span):
        return jnp.concatenate([ends[0, quad, span, :], ends[1, quad, span, :]], axis=1)

    def store(ref):
        def put(span, value):
            ref[span, :] = value

        return put

    standard_rows(both, mat_ref, work, corr, [store(first), store(last)])
    keep.wait()


def row_scratch(cols):
    return [
        pltpu.VMEM((GROUPS, CHUNK, 2 * cols), jnp.bfloat16),
        pltpu.VMEM((GROUPS, CHUNK, 2 * cols), jnp.float32),
    ]


def border(patterns, scan_mask, matrices):
    pixels, rows, cols = patterns.shape
    bf16 = jnp.bfloat16
    return pl.pallas_call(
        border_kernel,
        in_specs=[APART] * 3,
        out_specs=(APART, WHOLE, WHOLE, WHOLE),
        out_shape=(
            pltpu.HBM((rows - 2, GROUPS, CHUNK, cols), bf16),
            pltpu.VMEM((pixels, cols), bf16),
            pltpu.VMEM((pixels, cols), bf16),
            TOKEN,
        ),
        scratch_shapes=[
            pltpu.VMEM((rows, cols), scan_mask.dtype),
            pltpu.VMEM(matrices.shape, bf16),
            pltpu.VMEM((rows - 2, GROUPS, CHUNK, cols), bf16),
            pltpu.VMEM((2, GROUPS, CHUNK, cols), bf16),
            pltpu.VMEM((SLOTS, CHUNK, rows, cols), bf16),
        ]
        + row_scratch(cols)
        + [pltpu.SemaphoreType.DMA((SLOTS + 3,))],
        compiler_params=pltpu.CompilerParams(vmem_limit_bytes=18 * MIB),
        cost_estimate=SHORT,
        name="border",
    )(in_hbm(patterns), in_hbm(scan_mask), in_hbm(matrices))


def interior_kernel(xq_hbm, mat_hbm, *refs):
    s_ref, token, mat_ref, xq, buffer, corr, sems = refs[-7:]
    mark(token)
    pairs = s_ref.shape[0] // 2
    matrices = pltpu.make_async_copy(mat_hbm, mat_ref, sems.at[2])

    def fetch(i):
        slot = i % 2
        return pltpu.make_async_copy(xq_hbm.at[pl.ds(2 * i, 2)], xq.at[slot], sems.at[slot])

    fetch(0).start()
    matrices.start()
    if pairs > 1:
        fetch(1).start()
    matrices.wait()

    def work(source, at):
        def both(quad, span):
            return jnp.concatenate([source[0, quad, span, :], source[1, quad, span, :]], axis=1)

        def store(side):
            def put(span, value):
                s_ref[at + side, span, :] = value

            return put

        standard_rows(both, mat_ref, buffer, corr, [store(0), store(1)])

    for i in range(pairs):
        fetch(i).wait()
        work(xq.at[i % 2], 2 * i)
        if i + 2 < pairs:
            fetch(i + 2).start()


def interior(xq, matrices, *earlier):
    rows, _, _, cols = xq.shape
    pixels = GROUPS * CHUNK
    return pl.pallas_call(
        interior_kernel,
        in_specs=[APART, APART] + [APART] * len(earlier),
        out_specs=(WHOLE, WHOLE),
        out_shape=(pltpu.VMEM((rows, pixels, cols), jnp.bfloat16), TOKEN),
        scratch_shapes=[
            pltpu.VMEM(matrices.shape, jnp.bfloat16),
            pltpu.VMEM((2, 2, GROUPS, CHUNK, cols), jnp.bfloat16),
        ]
        + row_scratch(cols)
        + [pltpu.SemaphoreType.DMA((3,))],
        compiler_params=pltpu.CompilerParams(vmem_limit_bytes=11 * MIB),
        cost_estimate=SHORT,
        name="interior",
    )(in_hbm(xq), in_hbm(matrices), *earlier)


def row_of(refs, rows):
    above, first, middle, last, below = refs

    def row(r):
        if 1 <= r < rows - 1:
            return middle.at[r - 1]
        return {-1: above, 0: first, rows - 1: last, rows: below}[r]

    return row


def fetch_halo(refs, halo, sems):
    copies = [
        pltpu.make_async_copy(refs[0], halo.at[0], sems.at[0]),
        pltpu.make_async_copy(refs[4], halo.at[1], sems.at[1]),
    ]
    for copy in copies:
        copy.start()
    return (halo.at[0], refs[1], refs[2], refs[3], halo.at[1]), [copy.wait for copy in copies]


HALO = pl.BlockSpec(memory_space=pl.ANY)
BLOCK = [HALO, WHOLE, WHOLE, WHOLE, HALO]


def halo_scratch(pixels, cols):
    return [pltpu.VMEM((2, pixels, cols), jnp.bfloat16), pltpu.SemaphoreType.DMA((2,))]


def on_chip_but_halo(block):
    return [block[0], *map(on_chip, block[1:4]), block[4]]


def diagonals(product, at_sub, at_lane):
    return [
        jnp.sum(jnp.where(at_sub == at_lane + d, product, 0.0), axis=0, keepdims=True)
        for d in (-1, 0, 1)
    ]


PER_ROW = 8


def products_kernel(*refs):
    left, right, out, halo, sems = refs[-5:]
    rows = refs[2].shape[0] + 2
    cols = refs[1].shape[1]
    block, waits = fetch_halo(refs[:5], halo, sems)
    row = row_of(block, rows)
    f32 = jnp.float32
    at_sub = lax.broadcasted_iota(jnp.int32, (cols, cols), 0)
    at_lane = lax.broadcasted_iota(jnp.int32, (cols, cols), 1)
    firsts, lasts = {}, {}
    for r in [*range(rows - 1), rows - 1, rows, -1]:
        if r == rows - 1:
            waits[1]()
        if r == -1:
            waits[0]()
        here = row(r)[...]
        across = here.T
        firsts[r] = across[:1]
        lasts[r] = across[cols - 1 :]
        pieces = [here]
        if r < rows:
            pieces.append(row(r + 1)[...])
        product = jnp.dot(across, jnp.concatenate(pieces, axis=1), preferred_element_type=f32)
        own = diagonals(product[:, :cols], at_sub, at_lane)
        vectors = [own[1], own[0]]
        if r < rows:
            vectors += diagonals(product[:, cols:], at_sub, at_lane)
        vectors += [jnp.zeros((1, cols), f32)] * (PER_ROW - len(vectors))
        out[r + 1] = jnp.concatenate(vectors, axis=0)
    blank = [jnp.zeros((SIDES // 2 - len(firsts), here.shape[0]), here.dtype)]
    order = range(-1, rows + 1)
    left[...] = jnp.concatenate([firsts[r] for r in order] + blank, axis=0)
    right[...] = jnp.concatenate([lasts[r] for r in order] + blank, axis=0)


def products(block, *earlier):
    rows = block[2].shape[0] + 2
    pixels, cols = block[0].shape
    one = jax.ShapeDtypeStruct((SIDES // 2, pixels), jnp.bfloat16)
    return pl.pallas_call(
        products_kernel,
        in_specs=BLOCK + [APART] * len(earlier),
        out_specs=(WHOLE,) * 3,
        out_shape=(one, one, jax.ShapeDtypeStruct((rows + 2, PER_ROW, cols), jnp.float32)),
        scratch_shapes=halo_scratch(pixels, cols),
        compiler_params=pltpu.CompilerParams(vmem_limit_bytes=6 * MIB),
        cost_estimate=SHORT,
        name="products",
    )(*on_chip_but_halo(block), *earlier)


def average_kernel(*refs):
    left_ref, right_ref, own_left_ref, own_right_ref, dot_ref, usable_ref = refs[5:11]
    a_ref, inv_ref, sides, weights, halo, sems = refs[-6:]
    rows, pixels, cols = a_ref.shape
    block, waits = fetch_halo(refs[:5], halo, sems)
    row = row_of(block, rows)
    f32 = jnp.float32
    at_sub = lax.broadcasted_iota(jnp.int32, (cols, cols), 0)
    at_lane = lax.broadcasted_iota(jnp.int32, (cols, cols), 1)
    lane = lax.broadcasted_iota(jnp.int32, (1, cols), 1)

    pad = jnp.zeros((LANES, cols - SIDES), f32)
    for start in range(0, pixels, LANES):
        width = min(LANES, pixels - start)
        span = slice(start, start + width)
        piece = jnp.concatenate([left_ref[:, span], right_ref[:, span]], axis=0).astype(f32)
        sides[span, :] = jnp.concatenate([piece.T, pad[:width]], axis=1).astype(jnp.bfloat16)

    meet = []
    for own, halo in ((own_left_ref, left_ref), (own_right_ref, right_ref)):
        both = jnp.concatenate([own[...], halo[...]], axis=0)
        meet.append(
            lax.dot_general(both, halo[...], (((1,), (1,)), ((), ())), preferred_element_type=f32)
        )

    def shifted(vector, dc):
        if dc == 0:
            return vector
        return pltpu.roll(vector, (-dc) % cols, 1)

    def kept(r, k):
        return dot_ref[r + 1, pl.ds(k, 1), :]

    for r in [*range(1, rows - 1), 0, rows - 1]:
        if r == 0:
            waits[0]()
        if r == rows - 1:
            waits[1]()
        weight = {}
        slot = 0
        total = jnp.ones((1, cols), f32)
        for dr in (-1, 0, 1):
            for dc in (-1, 0, 1):
                if dr == 0 and dc == 0:
                    continue
                if dr == -1:
                    dot = kept(r - 1, 3 + dc)
                elif dr == 1:
                    dot = shifted(kept(r, 3 - dc), dc)
                else:
                    dot = kept(r, 1) if dc == -1 else shifted(kept(r, 1), 1)
                other = shifted(kept(r + dr, 0), dc)
                if dc != 0:
                    k, near = r + dr + 1, meet[0 if dc < 0 else 1]
                    end = 0 if dc < 0 else cols - 1
                    half = SIDES // 2
                    dot = jnp.where(lane == end, near[r + 1 : r + 2, k : k + 1], dot)
                    other = jnp.where(lane == end, near[half + k : half + k + 1, k : k + 1], other)
                distance = jnp.maximum(kept(r, 0) + other - 2.0 * dot, 0.0) / pixels
                weight[dr, dc] = usable_ref[slot, pl.ds(r, 1), :] * jnp.exp(-distance / nlpar_scale)
                total = total + weight[dr, dc]
                slot += 1
        for dr in (-1, 0, 1):
            block = jnp.zeros((cols, cols), f32)
            for dc in (-1, 0, 1):
                w = jnp.ones((1, cols), f32) if dr == 0 and dc == 0 else weight[dr, dc]
                block = jnp.where(at_sub == at_lane + dc, w, block)
            weights[dr + 1] = block
        block = jnp.zeros((cols, cols), f32)
        for dr in (-1, 0, 1):
            for dc in (-1, 1):
                k = r + dr + 1 + (0 if dc < 0 else 16)
                end = 0 if dc < 0 else cols - 1
                block = jnp.where((at_sub == k) & (at_lane == end), weight[dr, dc], block)
        weights[3] = block

        full = weights[...].reshape(4 * cols, cols)
        high = full.astype(jnp.bfloat16)
        low = (full - high.astype(f32)).astype(jnp.bfloat16)
        split = jnp.concatenate([high, low], axis=1)
        inverse = 1.0 / total
        squares = jnp.zeros((8, cols), f32)
        for g in range(GROUPS):
            span = slice(g * CHUNK, (g + 1) * CHUNK)
            lhs = jnp.concatenate(
                [row(r - 1)[span, :], row(r)[span, :], row(r + 1)[span, :], sides[span, :]], axis=1
            )
            out = jnp.dot(lhs, split, preferred_element_type=f32)
            mean = ((out[:, :cols] + out[:, cols:]) * inverse).astype(jnp.bfloat16)
            a_ref[r, span, :] = mean
            mean32 = mean.astype(f32).reshape(CHUNK // 8, 8, cols)
            squares = squares + jnp.sum(mean32 * mean32, axis=0)
        energy = jnp.sum(squares, axis=0, keepdims=True) / pixels
        inv_ref[pl.ds(r, 1), :] = 1.0 / jnp.sqrt(energy + epsilon)


def average(block, left, right, own_left, own_right, dots, usable, *earlier):
    rows = block[2].shape[0] + 2
    pixels, cols = block[0].shape
    return pl.pallas_call(
        average_kernel,
        in_specs=BLOCK + [WHOLE] * 6 + [APART] * len(earlier),
        out_specs=(WHOLE, WHOLE),
        out_shape=(
            pltpu.VMEM((rows, pixels, cols), jnp.bfloat16),
            jax.ShapeDtypeStruct((rows, cols), jnp.float32),
        ),
        scratch_shapes=[
            pltpu.VMEM((pixels, cols), jnp.bfloat16),
            pltpu.VMEM((4, cols, cols), jnp.float32),
        ]
        + halo_scratch(pixels, cols),
        compiler_params=pltpu.CompilerParams(vmem_limit_bytes=6 * MIB),
        cost_estimate=SHORT,
        name="average",
    )(*on_chip_but_halo(block), left, right, own_left, own_right, dots, usable, *earlier)


def insert(best, new):
    kept = []
    for slot, held in enumerate(best):
        kept.append(jnp.maximum(held, new))
        if slot < len(best) - 1:
            new = jnp.minimum(held, new)
    return kept


def merge_sublanes(best):
    for shift in (4, 2, 1):
        other = [pltpu.roll(b, shift, 0) for b in best]
        m = [jnp.maximum(best[i], other[3 - i]) for i in range(4)]
        a, c = jnp.maximum(m[0], m[2]), jnp.minimum(m[0], m[2])
        b, d = jnp.maximum(m[1], m[3]), jnp.minimum(m[1], m[3])
        best = [jnp.maximum(a, b), jnp.minimum(a, b), jnp.maximum(c, d), jnp.minimum(c, d)]
    return best


def score_kernel(count, a_ref, best_ref, *refs):
    pieces, last = refs[:count], refs[count:]
    out = last[-1]
    rows, pixels, cols = a_ref.shape
    f32 = jnp.float32
    panels = pieces[0].shape[0]
    entries = jnp.concatenate([piece[k] for k in range(panels) for piece in pieces], axis=0)
    each = sum(piece.shape[1] for piece in pieces)
    entries32 = entries.astype(f32)
    energy = jnp.sum(entries32 * entries32, axis=1, keepdims=True) / pixels
    inv_entry = 1.0 / jnp.sqrt(energy + epsilon) / pixels
    for r in range(0, rows, 2):
        block = jnp.concatenate([a_ref[r], a_ref[r + 1]], axis=1)
        scores = jnp.dot(entries, block, preferred_element_type=f32) * inv_entry
        for k in range(panels):
            for half in range(2):
                held = [best_ref[k, j, r + half] for j in range(TOP)]
                for e in range(k * each, (k + 1) * each, 8):
                    held = insert(held, scores[e : e + 8, half * cols : (half + 1) * cols])
                if len(last) > 1:
                    inv = last[0][pl.ds(r + half, 1), :]
                    held = merge_sublanes(held)
                    for j in range(TOP):
                        out[k, j, pl.ds(r + half, 1), :] = held[j][:1] * inv
                else:
                    for j in range(TOP):
                        out[k, j, r + half] = held[j]


def score(averaged, best, pieces, inv_pattern=None):
    last = [] if inv_pattern is None else [inv_pattern]
    panels, top, rows, sublanes, cols = best.shape
    shape = (panels, top, rows, cols) if last else best.shape
    out = jax.ShapeDtypeStruct(shape, jnp.float32) if last else pltpu.VMEM(shape, jnp.float32)
    return pl.pallas_call(
        functools.partial(score_kernel, len(pieces)),
        in_specs=[WHOLE] * (2 + len(pieces) + len(last)),
        out_specs=WHOLE,
        out_shape=out,
        compiler_params=pltpu.CompilerParams(vmem_limit_bytes=2 * MIB),
        cost_estimate=SHORT,
        name="score",
    )(on_chip(averaged), on_chip(best), *pieces, *last)


def exchange(x, axis, masks):
    count = lax.axis_size(axis)
    return lax.ppermute(x, axis, [(i, i ^ masks[i & 1]) for i in range(count)])


def power_of_two(n):
    return n & (n - 1) == 0


def hold(x, *earlier):
    def nothing(*refs):
        pass

    return pl.pallas_call(
        nothing,
        in_specs=[APART] + [APART] * len(earlier),
        out_specs=APART,
        out_shape=jax.ShapeDtypeStruct(x.shape, x.dtype),
        input_output_aliases={0: 0},
        compiler_params=pltpu.CompilerParams(vmem_limit_bytes=MIB // 8),
        cost_estimate=SHORT,
        name="hold",
    )(x, *earlier)


def join_kernel(count, *refs):
    parts, (out, token, sems) = refs[:count], refs[-3:]
    mark(token)
    copies, at = [], 0
    for i, part in enumerate(parts):
        size = part.shape[1]
        copies.append(pltpu.make_async_copy(part, out.at[:, pl.ds(at, size)], sems.at[i]))
        at += size
    for copy in copies:
        copy.start()
    for copy in copies:
        copy.wait()


def join(parts, *earlier):
    panels, _, pixels = parts[0].shape
    if any(part.shape[1] % 16 for part in parts):
        whole = jnp.concatenate(parts, axis=1)
        return hold(whole, *earlier), jnp.zeros(TOKEN.shape, TOKEN.dtype)
    size = sum(part.shape[1] for part in parts)
    return pl.pallas_call(
        functools.partial(join_kernel, len(parts)),
        in_specs=[APART] * len(parts) + [APART] * len(earlier),
        out_specs=(APART, WHOLE),
        out_shape=(jax.ShapeDtypeStruct((panels, size, pixels), parts[0].dtype), TOKEN),
        scratch_shapes=[pltpu.SemaphoreType.DMA((len(parts),))],
        compiler_params=pltpu.CompilerParams(vmem_limit_bytes=MIB // 8),
        cost_estimate=SHORT,
        name="join",
    )(*parts, *earlier)


def gathers(strip, line):
    return power_of_two(strip) and power_of_two(line) and strip > 2 and line > 1


def line_masks(line):
    return [line - 1] + [1 << i for i in range(line.bit_length() - 2)]


def strip_masks(strip):
    bits = [1 << i for i in range(1, strip.bit_length() - 1)]
    return list(zip(bits, reversed(bits)))


def from_low(x, axis):
    count = lax.axis_size(axis)
    return lax.ppermute(x, axis, [(i, i + 1) for i in range(count - 1)])


def from_high(x, axis):
    count = lax.axis_size(axis)
    return lax.ppermute(x, axis, [(i + 1, i) for i in range(count - 1)])


def usable_neighbours(neighbour_mask):
    _, rows, cols = neighbour_mask.shape
    row_at = lax.axis_index("strip") * rows + jnp.arange(rows, dtype=jnp.int32)
    col_at = lax.axis_index("dict") * cols + jnp.arange(cols, dtype=jnp.int32)
    all_rows = rows * lax.axis_size("strip")
    all_cols = cols * lax.axis_size("dict")
    inside = []
    for dr in (-1, 0, 1):
        for dc in (-1, 0, 1):
            if dr == 0 and dc == 0:
                continue
            row_ok = (row_at + dr >= 0) & (row_at + dr < all_rows)
            col_ok = (col_at + dc >= 0) & (col_at + dc < all_cols)
            inside.append(row_ok[:, None] & col_ok[None, :])
    return (jnp.stack(inside) & (neighbour_mask == 1)).astype(jnp.float32)


def on_device(patterns, scan_mask, neighbour_mask, dictionary):
    rows, cols = scan_mask.shape
    strip, line = lax.axis_size("strip"), lax.axis_size("dict")
    alone = not gathers(strip, line)
    matrices = jnp.asarray(pass_matrices())
    usable = usable_neighbours(neighbour_mask)
    best = jnp.full((dictionary.shape[0], TOP, rows, 8, cols), -jnp.inf, jnp.float32)
    if not alone:
        ways = strip_masks(strip)
        near = held = dictionary
        mirrored, *masks = line_masks(line)
        far = [exchange(held, "dict", (mirrored, mirrored))]
        near_new = exchange(near, "strip", ways[0])

    xq, first, last, bordered = border(patterns, scan_mask, matrices)
    above = from_low(last, "strip")
    below = from_high(first, "strip")
    middle, filled = interior(xq, matrices, bordered)
    block = (above, first, middle, last, below)
    if not alone:
        for mask in masks:
            held, _ = join([held, far[-1]], filled)
            far.append(exchange(held, "dict", (mask, mask)))

    own_left, own_right, dots = products(block)
    left = from_low(own_right, "dict")
    right = from_high(own_left, "dict")
    joined = []
    if not alone:
        far, done = join(far, dots)
        far_new = exchange(far, "strip", ways[0])
        for way in ways[1:]:
            far, done = join([far, far_new], left, right)
            far_new = exchange(far, "strip", way)
        joined = [done]
        for way in ways[1:]:
            near, done = join([near, near_new], done)
            near_new = exchange(near, "strip", way)
        joined.append(done)

    averaged, inv_pattern = average(block, left, right, own_left, own_right, dots, usable, *joined)
    if alone:
        whole = lax.all_gather(dictionary, ("strip", "dict"), axis=1, tiled=True)
        return score(averaged, best, [whole], inv_pattern)
    near, _ = join([near, near_new], inv_pattern)
    near_other = exchange(near, "strip", (1, 1))
    far_other = exchange(far, "strip", (1, 1))
    best = score(averaged, best, [far, far_other])
    best = score(averaged, best, [near, near_other])
    far_new = hold(far_new, best)
    far_new_other = exchange(far_new, "strip", (1, 1))
    best = score(averaged, best, [far_new])
    return score(averaged, best, [far_new_other], inv_pattern)


def solution(mesh):
    in_specs = (
        P(None, "strip", "dict"),
        P("strip", "dict"),
        P(None, "strip", "dict"),
        P(None, ("strip", "dict"), None),
    )
    out_specs = P(None, None, "strip", "dict")
    return jax.shard_map(
        on_device, mesh=mesh, in_specs=in_specs, out_specs=out_specs, check_vma=False
    )
```
